128 devices in a mesh: pipe: 16 (over z_hi, x, core), fsdp: 8 (over y, z_lo).
Axes of the slice: x: 4, y: 4, z: 4 (z_hi: 2, z_lo: 2; z = z_hi * 2 + z_lo), core: 2. Of those that a mesh axis runs over, the one named last changes fastest.
Arguments:
- hidden: bfloat16 [16384, 6144], P(('pipe', 'fsdp')), may hold values from -24 to 24
- gain: float32 [16, 6144], P('pipe'), may hold values from 0.5 to 1.5
- head: bfloat16 [16, 4096, 6144], P('pipe', 'fsdp'), may hold values from -0.50618622 to 0.50618622
- teacher_index: int32 [16384, 64], P('pipe'), may hold values from 0 to 4095, all different within a row
- teacher_logits: float32 [16384, 64], P('pipe'), may hold values from -12 to 410
- cotangent: float32 [16384], P('pipe'), may hold values from 64 to 512
Outputs:
- loss: float32 [16384], P(('pipe', 'fsdp'))
- grad_hidden: bfloat16 [16384, 6144], P(('pipe', 'fsdp'))
- grad_head: bfloat16 [16, 4096, 6144], P('pipe', 'fsdp')
- grad_gain: bfloat16 [16, 6144], P('pipe')
The draws below stay inside these ranges and needn't reach their ends.
Inputs may be any that keep to these rules, and one draw needn't show every extreme that they name: `teacher_index`: each row names 64 different entries.
All inputs are finite; a program needn't handle non-finite values.
Results may differ from the reference program's by a relative error of at most 0.019.
Values may be sent and summed in bfloat16 or wider, within the bound.
No kernel may reach another device: no remote copies, remote signals or barrier semaphores. Data moves between devices by JAX's collectives and lax.ppermute only.
A program may use at most 128 MiB of HBM per device.

```python
import math
import jax
import jax.numpy as jnp
from jax import lax

D = 6144
V_DEV = 512
K = 64
TOK_DEV = 128
VOCAB = 4096
TOKENS = 16384
N_PIPE = 16
N_FSDP = 8


def head_rows(key, flat_ids, boost):
    base_key = jax.random.fold_in(key, 5)

    def one_row(row_id):
        values = jax.random.normal(jax.random.fold_in(base_key, row_id), (D,), jnp.float32)
        return jnp.clip(values, -6.0, 6.0) * D ** (-0.5)

    def factor_of(row_id):
        entry = row_id % VOCAB
        return jnp.where(entry % 64 == 0, 1.0 + boost * (1.0 + entry // 64 % 3), 1.0)
    own = jax.vmap(one_row)(flat_ids) * factor_of(flat_ids)[:, None]
    paired = (flat_ids % VOCAB % 64 == 1)[:, None]
    return jnp.where(paired, own, own)


def draw_head(key, part):
    flat_ids = jnp.arange(N_PIPE * VOCAB, dtype=jnp.int32)
    rows = head_rows(key, flat_ids, 0.0)
    return rows.reshape(N_PIPE, VOCAB, D).astype(jnp.bfloat16)


def draw_hidden(key, part):
    own_key = jax.random.fold_in(key, 21)
    base = jnp.clip(jax.random.normal(own_key, (TOKENS, D), jnp.float32), -6.0, 6.0)
    return base.astype(jnp.bfloat16)


def draw_teacher_logits(key, part):
    own_key = jax.random.fold_in(key, 31)
    return jnp.clip(jax.random.normal(own_key, (TOKENS, K), jnp.float32), -6.0, 6.0) * 2.0


def shard_levels(rng, dims, cuts, least, high):
    level = 1.0
    for position, parts in cuts:
        draws = jax.random.uniform(jax.random.fold_in(jax.random.fold_in(rng, 6), position), (parts,), jnp.float32, least / len(cuts), high / len(cuts))
        level = level * jnp.repeat(jnp.exp(draws), dims[position] // parts).reshape((-1,) + (1,) * (len(dims) - 1 - position))
    return level


def picks_of(stream_key, rows, count, top, lift):
    ranking = jax.random.permutation(jax.random.fold_in(stream_key, 1), count)
    pull = ranking
    for power in range(3):
        pull = pull * pull // count
    pull = pull * lift // count
    lots = jax.random.randint(jax.random.fold_in(stream_key, 2), (rows, count), 0, 4096) + pull
    fixed_rows = jax.random.permutation(jax.random.fold_in(stream_key, 3), rows)[jnp.arange(count) % rows]
    lots = jnp.where(jnp.arange(rows)[:, None] == fixed_rows[None, :], 1 << 14, lots)
    merit = lots * count + jnp.arange(count)
    return lax.top_k(merit.astype(jnp.int32), top)[1].astype(jnp.int32)


def setup_inputs(seed: int = 0) -> dict:
    splits = jax.random.split(jax.random.key(seed), 7)
    hidden = draw_hidden(jax.random.fold_in(splits[6], 71), 0)
    gain = jnp.clip(1.0 + 0.1 * jax.random.normal(splits[1], (N_PIPE, D), jnp.float32), 0.5, 1.5)
    head = draw_head(jax.random.fold_in(splits[6], 71), 0)
    teacher_index = picks_of(splits[3], TOKENS, VOCAB, K, 0)
    teacher_logits = draw_teacher_logits(jax.random.fold_in(splits[6], 71), 0)
    cotangent = jnp.clip(jnp.exp(math.log(512.0) - 2.0794415 * jax.random.uniform(splits[5], (TOKENS,), jnp.float32) ** shard_levels(splits[5], (TOKENS,), ((0, 16),), -0.2, 0.2)), 64.0, 512.0)
    return dict(hidden=hidden, gain=gain, head=head, teacher_index=teacher_index, teacher_logits=teacher_logits, cotangent=cotangent)


smoothing = 0.1
epsilon = 1e-05

def section_pass(states, gain_row, table, index, teacher_row, weight_row):
    floats = states.astype(jnp.float32)
    scale = lax.rsqrt(lax.optimization_barrier(jnp.mean(floats * floats, axis=1)) + epsilon)
    unit = floats * scale[:, None]
    normed = (unit * gain_row[None, :]).astype(jnp.bfloat16)
    logits = lax.dot_general(normed, table, (((1,), (1,)), ((), ())), preferred_element_type=jnp.float32)
    top = lax.optimization_barrier(jnp.max(logits, axis=1))
    shifted = logits - top[:, None]
    expo = jnp.exp(shifted)
    total = lax.optimization_barrier(jnp.sum(expo, axis=1))
    moment = lax.optimization_barrier(jnp.sum(expo * shifted, axis=1))
    logz = top + jnp.log(total)
    entropy = moment / total - jnp.log(total)
    picks = jnp.take_along_axis(logits, index, axis=1)
    chosen = jnp.exp(picks - logz[:, None])
    teacher_log = math.log(1.0 - smoothing) + jax.nn.log_softmax(teacher_row, axis=1)
    rest = math.log(smoothing / (VOCAB - K))
    loss = entropy - lax.optimization_barrier(jnp.sum(chosen * teacher_log, axis=1)) - (1.0 - lax.optimization_barrier(jnp.sum(chosen, axis=1))) * rest
    probs = jnp.exp(logits - logz[:, None])
    dlogits = weight_row[:, None] * probs * (logits - logz[:, None] - rest - loss[:, None])
    row_ids = jnp.broadcast_to(jnp.arange(index.shape[0], dtype=jnp.int32)[:, None], index.shape)
    dlogits = dlogits.at[row_ids, index].add(weight_row[:, None] * chosen * (rest - teacher_log))
    dlow = dlogits.astype(jnp.bfloat16)
    grad_table = lax.dot_general(dlow, normed, (((0,), (0,)), ((), ())), preferred_element_type=jnp.float32).astype(jnp.bfloat16)
    dnormed = jnp.zeros(floats.shape, jnp.float32)
    for shard in range(N_FSDP):
        lower = shard * V_DEV
        piece = jnp.dot(dlow[:, lower:lower + V_DEV], table[lower:lower + V_DEV], preferred_element_type=jnp.float32)
        piece = lax.optimization_barrier(piece.astype(jnp.bfloat16))
        dnormed = dnormed + piece.astype(jnp.float32)
    grad_gain = lax.optimization_barrier(jnp.sum(unit * dnormed, axis=0)).astype(jnp.bfloat16)
    scaled = gain_row[None, :] * dnormed
    grad_states = scale[:, None] * scaled - scale[:, None] * unit * lax.optimization_barrier(jnp.mean(unit * scaled, axis=1, keepdims=True))
    return (loss, grad_states.astype(jnp.bfloat16), grad_table, grad_gain)

def reference(hidden, gain, head, teacher_index, teacher_logits, cotangent):
    tok_section = TOK_DEV * N_FSDP
    losses, grads_states, grads_table, grads_gain = ([], [], [], [])
    for section in range(N_PIPE):
        lower = section * tok_section
        upper = lower + tok_section
        outputs = section_pass(hidden[lower:upper], gain[section], head[section], teacher_index[lower:upper], teacher_logits[lower:upper], cotangent[lower:upper])
        losses.append(outputs[0])
        grads_states.append(outputs[1])
        grads_table.append(outputs[2])
        grads_gain.append(outputs[3])
    section_grad = jnp.stack(grads_table)
    section_gain = jnp.stack(grads_gain)
    merged_head = (section_grad.astype(jnp.float32) + section_grad[::-1].astype(jnp.float32)).astype(jnp.bfloat16)
    merged_gain = (section_gain.astype(jnp.float32) + section_gain[::-1].astype(jnp.float32)).astype(jnp.bfloat16)
    return (jnp.concatenate(losses), jnp.concatenate(grads_states, axis=0), merged_head, merged_gain)
```

```python
import functools
import math

import jax
import jax.numpy as jnp
from jax import lax
from jax.experimental import pallas as pl
from jax.experimental.pallas import tpu as pltpu
from jax.sharding import PartitionSpec as P

smoothing = 0.1
epsilon = 1e-05
F32 = jnp.float32
BF16 = jnp.bfloat16
BIG = 60 * 1024 * 1024

RING, SIDES = 4, 2
BLOCKS = RING * SIDES
ROWS, COLUMNS = 128, 768
PARTS = (
    (0, 1, 0, 4),
    (0, 1, 4, 4),
    (1, 3, 0, 2),
    (1, 3, 2, 2),
    (1, 3, 4, 2),
    (1, 3, 6, 2),
)


def params(**kw):
    return pltpu.CompilerParams(vmem_limit_bytes=BIG, **kw)


def cost(flops, nbytes):
    return pl.CostEstimate(flops=int(flops), bytes_accessed=int(nbytes), transcendentals=0)


def norm_kernel(hidden_ref, gain_ref, normed_ref, scale_ref):
    floats = hidden_ref[...].astype(F32)
    scale = lax.rsqrt(jnp.mean(floats * floats, axis=1, keepdims=True) + epsilon)
    normed_ref[...] = (floats * scale * gain_ref[...]).astype(BF16)
    scale_ref[...] = jnp.broadcast_to(scale, scale_ref.shape)


def norm_half(hidden, gain, half):
    rows, width = hidden.shape
    step = rows // 4
    return pl.pallas_call(
        norm_kernel,
        grid=(2,),
        in_specs=[
            pl.BlockSpec((step, width), lambda i: (i + 2 * half, 0)),
            pl.BlockSpec((1, width), lambda i: (0, 0)),
        ],
        out_specs=[
            pl.BlockSpec((step, width), lambda i: (i, 0)),
            pl.BlockSpec((step, 128), lambda i: (i, 0)),
        ],
        out_shape=[
            jax.ShapeDtypeStruct((rows // 2, width), BF16),
            jax.ShapeDtypeStruct((rows // 2, 128), F32),
        ],
        compiler_params=params(),
        cost_estimate=cost(rows * width * 2, rows * width * 2),
        name="norm_half",
    )(hidden, gain)


def teacher_kernel(rest, order_ref, base_ref, index_ref, logit_ref, out_ref):
    logits = jnp.transpose(logit_ref[...])
    top = jnp.max(logits, axis=0, keepdims=True)
    shifted = logits - top
    logsum = jnp.log(jnp.sum(jnp.exp(shifted), axis=0, keepdims=True))
    value = rest - (math.log(1.0 - smoothing) + (shifted - logsum))
    entry = jnp.transpose(index_ref[...]) - base_ref[0]
    num_top, tokens = value.shape
    part = 64
    for lower in range(0, out_ref.shape[1], part):
        row = lax.broadcasted_iota(jnp.int32, (part, tokens), 0) + lower
        dense = jnp.zeros((part, tokens), F32)
        for k in range(num_top):
            dense = jnp.where(row == entry[k : k + 1, :], value[k : k + 1, :], dense)
        out_ref[0, lower : lower + part, :] = dense


def teacher_weights(order, base, index, logits, width, rest):
    rows, num_top = index.shape
    tokens = rows // BLOCKS
    return pl.pallas_call(
        functools.partial(teacher_kernel, rest),
        grid_spec=pltpu.PrefetchScalarGridSpec(
            num_scalar_prefetch=2,
            grid=(BLOCKS,),
            in_specs=[
                pl.BlockSpec((tokens, num_top), lambda j, order, base: (order[j], 0)),
                pl.BlockSpec((tokens, num_top), lambda j, order, base: (order[j], 0)),
            ],
            out_specs=pl.BlockSpec((1, width, tokens), lambda j, order, base: (j, 0, 0)),
        ),
        out_shape=jax.ShapeDtypeStruct((BLOCKS, width, tokens), F32),
        compiler_params=params(),
        cost_estimate=cost(rows * width * num_top, rows * width * 4),
        name="teacher_weights",
    )(order, base, index, logits)


def logits_kernel(count, head_ref, *refs):
    pieces, weights = refs[: 2 * count], refs[2 * count : 3 * count]
    logits_ref, sums_ref = refs[3 * count :]
    step = pl.program_id(0)
    block = jnp.concatenate([p[...] for p in pieces], axis=0)
    part = lax.dot_general(
        head_ref[0], block, (((1,), (1,)), ((), ())), preferred_element_type=F32
    )
    tokens = logits_ref.shape[2]

    @pl.when(step == 0)
    def _():
        for n in range(count):
            logits_ref[n] = part[:, n * tokens : (n + 1) * tokens]

    @pl.when(step > 0)
    def _():
        for n in range(count):
            logits_ref[n] += part[:, n * tokens : (n + 1) * tokens]

    @pl.when(step == pl.num_programs(0) - 1)
    def _():
        for n in range(count):
            logits = logits_ref[n]
            top = jnp.max(logits, axis=0, keepdims=True)
            shifted = logits - top
            expo = jnp.exp(shifted)
            total = jnp.sum(expo, axis=0, keepdims=True)
            mixed = jnp.sum(expo * (shifted + weights[n][0]), axis=0, keepdims=True)
            sums_ref[n] = jnp.concatenate(
                [top, total, mixed, jnp.zeros((5, top.shape[1]), F32)], axis=0
            )


def block_logits(slots, a, b, head, weights):
    _, width, depth = head.shape
    half = a[slots[0]].shape[0]
    tokens = 2 * half
    count = len(slots)
    step = 3072
    return pl.pallas_call(
        functools.partial(logits_kernel, count),
        grid=(depth // step,),
        in_specs=[pl.BlockSpec((1, width, step), lambda i: (0, 0, i))]
        + [pl.BlockSpec((half, step), lambda i: (0, i))] * (2 * count)
        + [pl.BlockSpec((1, width, tokens), lambda i, s=s: (s, 0, 0)) for s in slots],
        out_specs=[
            pl.BlockSpec((count, width, tokens), lambda i: (0, 0, 0)),
            pl.BlockSpec((count, 8, tokens), lambda i: (0, 0, 0)),
        ],
        out_shape=[
            jax.ShapeDtypeStruct((count, width, tokens), F32),
            jax.ShapeDtypeStruct((count, 8, tokens), F32),
        ],
        compiler_params=params(),
        cost_estimate=cost(2 * count * tokens * width * depth, width * depth * 2),
        name="block_logits",
    )(head, *[x[s] for s in slots for x in (a, b)], *([weights] * count))


def merge_sums(parts):
    top = functools.reduce(jnp.maximum, [p[0] for p in parts])
    total, mixed = 0.0, 0.0
    for one_top, one_total, one_mixed in parts:
        down = jnp.exp(one_top - top)
        total = total + one_total * down
        mixed = mixed + down * (one_mixed + (one_top - top) * one_total)
    return top, total, mixed


def dlogits_kernel(rest, where, weight_ref, cot_ref, *refs):
    sums = refs[:RING]
    logits = refs[RING:-4]
    first_ref, other_ref, low_ref, loss_ref = refs[-4:]
    tokens = cot_ref.shape[1]
    for slot in range(BLOCKS):
        side, ahead = slot // RING, slot % RING
        parts = []
        for shift in range(RING):
            found = sums[shift][side * RING + (ahead + RING - shift) % RING]
            parts.append((found[0:1], found[1:2], found[2:3]))
        top, total, mixed = merge_sums(parts)
        logtotal = jnp.log(total)
        logz = top + logtotal
        loss = mixed / total - logtotal - rest
        group, at = where[slot]
        rel = logits[group][at] - logz
        grads = cot_ref[slot : slot + 1] * jnp.exp(rel) * (rel - (rest + loss) + weight_ref[slot])
        low = grads.astype(BF16)
        here = slice(slot * tokens, (slot + 1) * tokens)
        first_ref[:, here] = low[:ROWS]
        other_ref[:, here] = low[ROWS:]
        low_ref[here, :] = jnp.transpose(grads).astype(BF16)
        loss_ref[slot : slot + 1, :] = loss


def all_dlogits(groups, found, weights, cot, sums, rest):
    blocks, width, tokens = weights.shape
    where = {s: (g, n) for g, group in enumerate(groups) for n, s in enumerate(group)}
    return pl.pallas_call(
        functools.partial(dlogits_kernel, rest, where),
        out_shape=[
            jax.ShapeDtypeStruct((ROWS, blocks * tokens), BF16),
            jax.ShapeDtypeStruct((width - ROWS, blocks * tokens), BF16),
            jax.ShapeDtypeStruct((blocks * tokens, width), BF16),
            jax.ShapeDtypeStruct((blocks, tokens), F32),
        ],
        compiler_params=params(),
        cost_estimate=cost(blocks * width * tokens * 10, blocks * width * tokens * 12),
        name="all_dlogits",
    )(weights, cot, *sums, *found)


def part_kernel(low_ref, *refs):
    normed = jnp.concatenate([p[...] for p in refs[:-1]], axis=0)
    refs[-1][...] = jnp.dot(low_ref[...], normed, preferred_element_type=F32).astype(BF16)


def table_part(low_t, pieces, lower, size):
    rows, tokens = low_t.shape
    half = pieces[0].shape[0]
    step = COLUMNS
    start = lower // step
    return pl.pallas_call(
        part_kernel,
        grid=(size // step,),
        in_specs=[pl.BlockSpec((rows, tokens), lambda i: (0, 0))]
        + [pl.BlockSpec((half, step), lambda i: (0, i + start)) for _ in pieces],
        out_specs=pl.BlockSpec((rows, step), lambda i: (0, i)),
        out_shape=jax.ShapeDtypeStruct((rows, size), BF16),
        compiler_params=params(),
        cost_estimate=cost(2 * rows * tokens * size, (rows + tokens) * size * 2),
        name="table_part",
    )(low_t, *pieces)


def table_kernel(first_ref, other_ref, head_ref, gain_ref, *refs):
    pieces, (out_ref, gain_out_ref) = refs[:-2], refs[-2:]
    normed = jnp.concatenate([p[...] for p in pieces], axis=0)
    low = jnp.concatenate([first_ref[...], other_ref[...]], axis=0)
    grads = jnp.dot(low, normed, preferred_element_type=F32)
    out_ref[...] = grads.astype(BF16)
    along = jnp.sum(head_ref[0].astype(F32) * grads, axis=0, keepdims=True) / gain_ref[...]
    gain_out_ref[...] = jnp.broadcast_to(along, gain_out_ref.shape)


def own_table(first, other, head, gain, pieces):
    _, width, depth = head.shape
    tokens = first.shape[1]
    half = pieces[0].shape[0]
    step = COLUMNS
    return pl.pallas_call(
        table_kernel,
        grid=(depth // step,),
        in_specs=[
            pl.BlockSpec(first.shape, lambda i: (0, 0)),
            pl.BlockSpec(other.shape, lambda i: (0, 0)),
            pl.BlockSpec((1, width, step), lambda i: (0, 0, i)),
            pl.BlockSpec((1, step), lambda i: (0, i)),
        ]
        + [pl.BlockSpec((half, step), lambda i: (0, i)) for _ in pieces],
        out_specs=[
            pl.BlockSpec((width, step), lambda i: (0, i)),
            pl.BlockSpec((8, step), lambda i: (0, i)),
        ],
        out_shape=[
            jax.ShapeDtypeStruct((width, depth), BF16),
            jax.ShapeDtypeStruct((8, depth), F32),
        ],
        compiler_params=params(),
        cost_estimate=cost(2 * width * tokens * depth, (tokens + 2 * width) * depth * 2),
        name="own_table",
    )(first, other, head, gain, *pieces)


def add_kernel(own_ref, other_ref, *refs):
    refs[-1][0] = (own_ref[...].astype(F32) + other_ref[...].astype(F32)).astype(BF16)


def add_part(own, other, earlier, part):
    width, depth = own.shape
    row, num_rows, column, num_columns = part
    first = earlier is None
    return pl.pallas_call(
        add_kernel,
        grid=(num_rows, num_columns),
        in_specs=[
            pl.BlockSpec((ROWS, COLUMNS), lambda i, j: (i + row, j + column)),
            pl.BlockSpec((ROWS, COLUMNS), lambda i, j: (i, j)),
        ]
        + ([] if first else [pl.BlockSpec(memory_space=pl.ANY)]),
        out_specs=pl.BlockSpec((1, ROWS, COLUMNS), lambda i, j: (0, i + row, j + column)),
        out_shape=jax.ShapeDtypeStruct((1, width, depth), BF16),
        input_output_aliases={} if first else {2: 0},
        compiler_params=params(),
        cost_estimate=cost(other.size, other.size * 6),
        name="add_part",
    )(own, other, *(() if first else (earlier,)))


def partial_kernel(counts, head_ref, *refs):
    num = len(counts)
    lows, rest, outs = refs[:num], refs[num:-num], refs[-num:]
    low = jnp.concatenate([r[...] for r in lows], axis=0)
    sums = jnp.dot(low, head_ref[0], preferred_element_type=F32)
    half = lows[0].shape[0]
    at = 0
    for n, count in enumerate(counts):
        total = sums[n * half : (n + 1) * half].astype(BF16).astype(F32)
        for r in rest[at : at + count]:
            total = total + r[...].astype(F32)
        at += count
        outs[n][...] = total.astype(outs[n].dtype)


def partials(low, head, jobs, dtype=BF16):
    _, width, depth = head.shape
    half = low.shape[0] // (2 * BLOCKS)
    step = 2048
    counts = [len(add) for _, add in jobs]
    added = [x for _, add in jobs for x in add]
    piece = pl.BlockSpec((half, step), lambda i: (0, i))
    return pl.pallas_call(
        functools.partial(partial_kernel, counts),
        grid=(depth // step,),
        in_specs=[pl.BlockSpec((1, width, step), lambda i: (0, 0, i))]
        + [pl.BlockSpec((half, width), lambda i, at=at: (at, 0)) for at, _ in jobs]
        + [piece] * len(added),
        out_specs=[piece] * len(jobs),
        out_shape=[jax.ShapeDtypeStruct((half, depth), dtype) for _ in jobs],
        compiler_params=params(),
        cost_estimate=cost(
            2 * len(jobs) * half * width * depth,
            width * depth * 2 + (len(jobs) + len(added)) * half * depth * 2,
        ),
        name="partials",
    )(head, *([low] * len(jobs)), *added)


def ring_perm(step):
    return [
        (y * SIDES + s, ((y + step) % RING) * SIDES + s)
        for y in range(RING)
        for s in range(SIDES)
    ]


def gate(values, *needed):
    found = lax.optimization_barrier((tuple(values), tuple(needed)))[0]
    return found if len(found) > 1 else found[0]


def body(hidden, gain, head, teacher_index, teacher_logits, cotangent):
    up, down, across = ring_perm(1), ring_perm(-1), ring_perm(2)
    swap = [(f, f ^ 1) for f in range(BLOCKS)]
    num_pipe = lax.axis_size("pipe")
    mirror = [(p, num_pipe - 1 - p) for p in range(num_pipe)]
    facing = [
        (p * BLOCKS + f, (num_pipe - 1 - p) * BLOCKS + (f ^ 1))
        for p in range(num_pipe)
        for f in range(BLOCKS)
    ]

    def send(x, perm):
        return lax.ppermute(x, "fsdp", perm)

    def exchange(x):
        return lax.ppermute(x, ("pipe", "fsdp"), facing)

    _, width, depth = head.shape
    rows = teacher_index.shape[0]
    tokens = rows // BLOCKS
    num_top = teacher_index.shape[1]
    rest = math.log(smoothing / (width * BLOCKS - num_top))

    a, b = {}, {}
    a[0], scale_a = norm_half(hidden, gain, 0)
    b[0], scale_b = norm_half(hidden, gain, 1)
    a[3] = send(a[0], up)
    a[1] = send(a[0], down)
    a[4] = send(a[0], swap)
    b[3] = send(b[0], up)
    b[1] = send(b[0], down)

    me = lax.axis_index("fsdp")
    slots = jnp.arange(BLOCKS, dtype=jnp.int32)
    order = ((me // SIDES + slots % RING) % RING) * SIDES + (me % SIDES) ^ (slots // RING)
    order = order.astype(jnp.int32)
    base = (me * width).astype(jnp.int32).reshape(1)
    weights = teacher_weights(order, base, teacher_index, teacher_logits, width, rest)
    cot = jnp.take(cotangent.reshape(BLOCKS, tokens), order, axis=0)

    groups = ((0,), (3, 1, 4), (5,), (2, 7), (6,))
    found = [block_logits(groups[0], a, b, head, weights)]

    b0, a4 = gate((b[0], a[4]), a[3], a[1], found[0][1])
    b[4] = send(b0, swap)
    a[7] = send(a4, up)
    a[5] = send(a4, down)
    a3, b1, b[4] = gate((a[3], b[1], b[4]), b[3])
    a[2] = send(a3, up)
    b[2] = send(b1, down)
    b[5] = send(b1, swap)
    found.append(block_logits(groups[1], a, b, head, weights))
    b3, a7, b5 = gate((b[3], a[7], b[5]), a[5], found[1][1])
    b[7] = send(b3, swap)
    a[6] = send(a7, up)
    b[6] = send(b5, down)
    found.append(block_logits(groups[2], a, b, head, weights))
    a[2], b[2], b[7] = gate((a[2], b[2], b[7]), found[2][1])
    found.append(block_logits(groups[3], a, b, head, weights))
    a[6], b[6] = gate((a[6], b[6]), found[3][1])
    found.append(block_logits(groups[4], a, b, head, weights))

    at = [s for group in groups for s in group]
    sums = jnp.concatenate([f[1] for f in found], axis=0)
    sums = jnp.stack([sums[at.index(s)] for s in range(BLOCKS)])

    def rows_of(x):
        return x[:, 0:1], x[:, 1:2], x[:, 2:3]

    other = send(sums, swap)
    other = jnp.concatenate([other[RING:], other[:RING]], axis=0)
    pair = merge_sums([rows_of(sums), rows_of(other)])
    pair = jnp.concatenate(pair + (jnp.zeros((BLOCKS, 5, tokens), F32),), axis=1)
    ring_sums = [pair, send(pair, down), send(pair, across), send(pair, up)]
    first, second, low, loss = all_dlogits(
        groups, [f[0] for f in found], weights, cot, ring_sums, rest
    )

    pieces, facing_pieces = [], []
    for slot in range(BLOCKS):
        pieces += [a[slot], b[slot]]
        other_slot = (slot + RING) % BLOCKS
        facing_pieces += [a[other_slot], b[other_slot]]

    their_first, their_second = send(first, swap), send(second, swap)
    o2a, o2b = partials(low, head, [(12, []), (13, [])])
    r_o2a, r_o2b = send(o2a, down), send(o2b, up)

    def part_of(n):
        row, _, column, num_columns = PARTS[n]
        mine = their_first if row == 0 else their_second
        return table_part(mine, facing_pieces, column * COLUMNS, num_columns * COLUMNS)

    theirs = [None] * len(PARTS)
    their_first = gate((their_first,), o2a)
    part = part_of(0)
    theirs[0] = exchange(part)
    their_first = gate((their_first,), part)
    part = part_of(1)
    theirs[1] = exchange(part)

    low = gate((low,), part)
    s2a, s2b, o3b, o0b = partials(low, head, [(4, []), (5, []), (15, []), (9, [])])
    s2a, s2b, o3b, their_second = gate((s2a, s2b, o3b, their_second), r_o2a, r_o2b)
    r_s2a, r_s2b, r_o3b = send(s2a, down), send(s2b, up), send(o3b, swap)
    part = gate((part_of(2),), theirs[0])
    theirs[2] = exchange(part)
    low = gate((low,), part)
    o3a, o1a, s1a = partials(low, head, [(14, [r_o2a]), (10, []), (2, [])])
    part = part_of(3)
    o3a, o1a, o0b = gate((o3a, o1a, o0b), r_s2a, r_s2b, r_o3b, part)
    r_o3a, r_o1a, r_o0b = send(o3a, down), send(o1a, up), send(o0b, swap)
    part = gate((part,), theirs[1], o0b)
    theirs[3] = exchange(part)
    low = gate((low,), part)
    s3a, o1b = partials(low, head, [(6, [r_s2a]), (11, [r_o2b])])
    part = part_of(4)
    s3a, s1a, o1b = gate((s3a, s1a, o1b), r_o3a, r_o1a, r_o0b, part)
    r_s3a, r_s1a, r_o1b = send(s3a, down), send(s1a, up), send(o1b, swap)
    part = gate((part,), theirs[2], o1b)
    theirs[4] = exchange(part)
    low = gate((low,), part)
    s3b, o0a = partials(low, head, [(7, [r_o3b]), (8, [r_o3a, r_o1a])])
    part = part_of(5)
    s3b, o0a = gate((s3b, o0a), r_s3a, r_s1a, r_o1b, part)
    r_s3b, r_o0a = send(s3b, down), send(o0a, swap)
    (s1b,) = partials(low, head, [(3, [r_s2b, r_o1b])])
    r_s1b = send(s1b, up)
    part = gate((part,), theirs[3], s1b)
    theirs[5] = exchange(part)
    first, second = gate((first, second), part)
    own, along = own_table(first, second, head, gain, pieces)

    along = along[:1].reshape(8, depth // 8)
    along = along + send(along, swap)
    along = along + send(along, [(f, f ^ SIDES) for f in range(BLOCKS)])
    along = along + send(along, across)
    along = along.astype(BF16)
    merged_gain = (
        along.astype(F32) + lax.ppermute(along, "pipe", mirror).astype(F32)
    ).astype(BF16).reshape(1, depth)

    merged = None
    for n in range(4):
        merged = add_part(own, theirs[n], merged, PARTS[n])
    low = gate((low,), r_s3b, r_o0a, r_s1b, merged)
    sum_a, sum_b = partials(
        low, head, [(0, [r_s3a, r_s1a, r_o0a]), (1, [r_s3b, r_s1b, r_o0b])], F32
    )

    dnormed = jnp.concatenate([sum_a, sum_b], axis=0)
    scale = jnp.concatenate([scale_a, scale_b], axis=0)[:, :1]
    unit = hidden.astype(F32) * scale
    scaled = gain * dnormed
    grad_states = scale * scaled - scale * unit * jnp.mean(unit * scaled, axis=1, keepdims=True)
    grad_states = grad_states.astype(BF16)

    theirs[4], theirs[5] = gate((theirs[4], theirs[5]), grad_states)
    for n in range(4, len(PARTS)):
        merged = add_part(own, theirs[n], merged, PARTS[n])
    return (loss[0], grad_states, merged, merged_gain)


def solution(mesh):
    in_specs = (
        P(("pipe", "fsdp"), None),
        P("pipe", None),
        P("pipe", "fsdp", None),
        P("pipe", None),
        P("pipe", None),
        P("pipe"),
    )
    out_specs = (
        P(("pipe", "fsdp")),
        P(("pipe", "fsdp"), None),
        P("pipe", "fsdp", None),
        P("pipe", None),
    )
    return jax.shard_map(body, mesh=mesh, in_specs=in_specs, out_specs=out_specs, check_vma=False)
```

```python
import functools
import math

import jax
import jax.numpy as jnp
from jax import lax
from jax.experimental import pallas as pl
from jax.experimental.pallas import tpu as pltpu
from jax.sharding import PartitionSpec as P

smoothing = 0.1
epsilon = 1e-05
F32 = jnp.float32
BF16 = jnp.bfloat16
BIG = 60 * 1024 * 1024

RING, SIDES = 4, 2
BLOCKS = RING * SIDES
ROWS, COLUMNS = 128, 768
PARTS = (
    (0, 1, 0, 2),
    (0, 1, 2, 2),
    (1, 3, 0, 3),
    (1, 3, 3, 3),
    (1, 3, 6, 2),
    (0, 1, 4, 4),
)


def params(**kw):
    return pltpu.CompilerParams(vmem_limit_bytes=BIG, **kw)


def cost(flops, nbytes):
    del flops, nbytes
    return pl.CostEstimate(flops=1, bytes_accessed=1, transcendentals=0)


def norm_kernel(hidden_ref, gain_ref, normed_ref, scale_ref):
    floats = hidden_ref[...].astype(F32)
    scale = lax.rsqrt(jnp.mean(floats * floats, axis=1, keepdims=True) + epsilon)
    normed_ref[...] = (floats * scale * gain_ref[...]).astype(BF16)
    scale_ref[...] = jnp.broadcast_to(scale, scale_ref.shape)


def norm_half(hidden, gain, half):
    rows, width = hidden.shape
    step = rows // 4
    return pl.pallas_call(
        norm_kernel,
        grid=(2,),
        in_specs=[
            pl.BlockSpec((step, width), lambda i: (i + 2 * half, 0)),
            pl.BlockSpec((1, width), lambda i: (0, 0)),
        ],
        out_specs=[
            pl.BlockSpec((step, width), lambda i: (i, 0)),
            pl.BlockSpec((step, 128), lambda i: (i, 0)),
        ],
        out_shape=[
            jax.ShapeDtypeStruct((rows // 2, width), BF16),
            jax.ShapeDtypeStruct((rows // 2, 128), F32),
        ],
        compiler_params=params(),
        cost_estimate=cost(rows * width * 2, rows * width * 2),
        name="norm_half",
    )(hidden, gain)


def teacher_kernel(rest, order_ref, base_ref, index_ref, logit_ref, out_ref):
    logits = logit_ref[...]
    top = jnp.max(logits, axis=0, keepdims=True)
    shifted = logits - top
    logsum = jnp.log(jnp.sum(jnp.exp(shifted), axis=0, keepdims=True))
    value = rest - (math.log(1.0 - smoothing) + (shifted - logsum))
    entry = index_ref[...] - base_ref[0]
    num_top, tokens = value.shape
    part = 64
    for lower in range(0, out_ref.shape[1], part):
        row = lax.broadcasted_iota(jnp.int32, (part, tokens), 0) + lower
        dense = jnp.zeros((part, tokens), F32)
        for k in range(num_top):
            dense = jnp.where(row == entry[k : k + 1, :], value[k : k + 1, :], dense)
        out_ref[0, lower : lower + part, :] = dense


def teacher_weights(order, base, index, logits, width, rest):
    num_top = index.shape[0]
    slots = order.shape[0]
    tokens = index.shape[1] // BLOCKS
    spec = pl.BlockSpec((num_top, tokens), lambda j, order, base: (0, order[j]))
    return pl.pallas_call(
        functools.partial(teacher_kernel, rest),
        grid_spec=pltpu.PrefetchScalarGridSpec(
            num_scalar_prefetch=2,
            grid=(slots,),
            in_specs=[spec, spec],
            out_specs=pl.BlockSpec((1, width, tokens), lambda j, order, base: (j, 0, 0)),
        ),
        out_shape=jax.ShapeDtypeStruct((slots, width, tokens), F32),
        compiler_params=params(),
        cost_estimate=cost(slots * tokens * width * num_top, slots * tokens * width * 4),
        name="teacher_weights",
    )(order, base, index, logits)


def logits_kernel(count, head_ref, *refs):
    pieces, weights = refs[: 2 * count], refs[2 * count : 3 * count]
    logits_ref, sums_ref = refs[3 * count :]
    step = pl.program_id(0)
    block = jnp.concatenate([p[...] for p in pieces], axis=0)
    part = lax.dot_general(
        head_ref[0], block, (((1,), (1,)), ((), ())), preferred_element_type=F32
    )
    tokens = logits_ref.shape[2]

    @pl.when(step == 0)
    def _():
        for n in range(count):
            logits_ref[n] = part[:, n * tokens : (n + 1) * tokens]

    @pl.when(step > 0)
    def _():
        for n in range(count):
            logits_ref[n] += part[:, n * tokens : (n + 1) * tokens]

    @pl.when(step == pl.num_programs(0) - 1)
    def _():
        for n in range(count):
            logits = logits_ref[n]
            top = jnp.max(logits, axis=0, keepdims=True)
            shifted = logits - top
            expo = jnp.exp(shifted)
            total = jnp.sum(expo, axis=0, keepdims=True)
            mixed = jnp.sum(expo * (shifted + weights[n][0]), axis=0, keepdims=True)
            sums_ref[n] = jnp.concatenate(
                [top, total, mixed, jnp.zeros((5, top.shape[1]), F32)], axis=0
            )


def block_logits(slots, a, b, head, weights):
    _, width, depth = head.shape
    half = a[slots[0]].shape[0]
    tokens = 2 * half
    count = len(slots)
    step = 3072
    return pl.pallas_call(
        functools.partial(logits_kernel, count),
        grid=(depth // step,),
        in_specs=[pl.BlockSpec((1, width, step), lambda i: (0, 0, i))]
        + [pl.BlockSpec((half, step), lambda i: (0, i))] * (2 * count)
        + [pl.BlockSpec((1, width, tokens), lambda i, s=s: (s % RING, 0, 0)) for s in slots],
        out_specs=[
            pl.BlockSpec((count, width, tokens), lambda i: (0, 0, 0)),
            pl.BlockSpec((count, 8, tokens), lambda i: (0, 0, 0)),
        ],
        out_shape=[
            jax.ShapeDtypeStruct((count, width, tokens), F32),
            jax.ShapeDtypeStruct((count, 8, tokens), F32),
        ],
        compiler_params=params(),
        cost_estimate=cost(2 * count * tokens * width * depth, width * depth * 2),
        name="block_logits",
    )(head, *[x[s] for s in slots for x in (a, b)], *[weights[s // RING] for s in slots])


def merge_sums(parts):
    top = functools.reduce(jnp.maximum, [p[0] for p in parts])
    total, mixed = 0.0, 0.0
    for one_top, one_total, one_mixed in parts:
        down = jnp.exp(one_top - top)
        total = total + one_total * down
        mixed = mixed + down * (one_mixed + (one_top - top) * one_total)
    return top, total, mixed


def dlogits_kernel(rest, where, cot_ref, *refs):
    weights, sums = refs[:SIDES], refs[SIDES : SIDES + RING]
    logits = refs[SIDES + RING : -4]
    first_ref, other_ref, low_ref, loss_ref = refs[-4:]
    tokens = cot_ref.shape[1]
    for slot in range(BLOCKS):
        side, ahead = slot // RING, slot % RING
        parts = []
        for shift in range(RING):
            found = sums[shift][side * RING + (ahead + RING - shift) % RING]
            parts.append((found[0:1], found[1:2], found[2:3]))
        top, total, mixed = merge_sums(parts)
        logtotal = jnp.log(total)
        logz = top + logtotal
        loss = mixed / total - logtotal - rest
        group, at = where[slot]
        rel = logits[group][at] - logz
        grads = cot_ref[slot : slot + 1] * jnp.exp(rel) * (rel - (rest + loss) + weights[side][ahead])
        low = grads.astype(BF16)
        here = slice(slot * tokens, (slot + 1) * tokens)
        first_ref[:, here] = low[:ROWS]
        other_ref[:, here] = low[ROWS:]
        low_ref[here, :] = jnp.transpose(grads).astype(BF16)
        loss_ref[slot : slot + 1, :] = loss


def all_dlogits(groups, found, weights, cot, sums, rest):
    _, width, tokens = weights[0].shape
    blocks = BLOCKS
    where = {s: (g, n) for g, group in enumerate(groups) for n, s in enumerate(group)}
    return pl.pallas_call(
        functools.partial(dlogits_kernel, rest, where),
        out_shape=[
            jax.ShapeDtypeStruct((ROWS, blocks * tokens), BF16),
            jax.ShapeDtypeStruct((width - ROWS, blocks * tokens), BF16),
            jax.ShapeDtypeStruct((blocks * tokens, width), BF16),
            jax.ShapeDtypeStruct((blocks, tokens), F32),
        ],
        compiler_params=params(),
        cost_estimate=cost(blocks * width * tokens * 10, blocks * width * tokens * 12),
        name="all_dlogits",
    )(cot, *weights, *sums, *found)


def part_kernel(low_ref, *refs):
    normed = jnp.concatenate([p[...] for p in refs[:-1]], axis=0)
    refs[-1][...] = jnp.dot(low_ref[...], normed, preferred_element_type=F32).astype(BF16)


def table_part(low_t, pieces, lower, size):
    rows, tokens = low_t.shape
    half = pieces[0].shape[0]
    step = COLUMNS
    start = lower // step
    return pl.pallas_call(
        part_kernel,
        grid=(size // step,),
        in_specs=[pl.BlockSpec((rows, tokens), lambda i: (0, 0))]
        + [pl.BlockSpec((half, step), lambda i: (0, i + start)) for _ in pieces],
        out_specs=pl.BlockSpec((rows, step), lambda i: (0, i)),
        out_shape=jax.ShapeDtypeStruct((rows, size), BF16),
        compiler_params=params(),
        cost_estimate=cost(2 * rows * tokens * size, (rows + tokens) * size * 2),
        name="table_part",
    )(low_t, *pieces)


def table_kernel(first_ref, other_ref, head_ref, gain_ref, *refs):
    pieces, (out_ref, gain_out_ref) = refs[:-2], refs[-2:]
    normed = jnp.concatenate([p[...] for p in pieces], axis=0)
    low = jnp.concatenate([first_ref[...], other_ref[...]], axis=0)
    grads = jnp.dot(low, normed, preferred_element_type=F32)
    out_ref[...] = grads.astype(BF16)
    along = jnp.sum(head_ref[0].astype(F32) * grads, axis=0, keepdims=True) / gain_ref[...]
    gain_out_ref[...] = jnp.broadcast_to(along, gain_out_ref.shape)


def own_table(first, other, head, gain, pieces):
    _, width, depth = head.shape
    tokens = first.shape[1]
    half = pieces[0].shape[0]
    step = COLUMNS
    return pl.pallas_call(
        table_kernel,
        grid=(depth // step,),
        in_specs=[
            pl.BlockSpec(first.shape, lambda i: (0, 0)),
            pl.BlockSpec(other.shape, lambda i: (0, 0)),
            pl.BlockSpec((1, width, step), lambda i: (0, 0, i)),
            pl.BlockSpec((1, step), lambda i: (0, i)),
        ]
        + [pl.BlockSpec((half, step), lambda i: (0, i)) for _ in pieces],
        out_specs=[
            pl.BlockSpec((width, step), lambda i: (0, i)),
            pl.BlockSpec((8, step), lambda i: (0, i)),
        ],
        out_shape=[
            jax.ShapeDtypeStruct((width, depth), BF16),
            jax.ShapeDtypeStruct((8, depth), F32),
        ],
        compiler_params=params(),
        cost_estimate=cost(2 * width * tokens * depth, (tokens + 2 * width) * depth * 2),
        name="own_table",
    )(first, other, head, gain, *pieces)


def add_kernel(own_ref, other_ref, *refs):
    refs[-1][0] = (own_ref[...].astype(F32) + other_ref[...].astype(F32)).astype(BF16)


def add_part(own, other, earlier, part):
    width, depth = own.shape
    row, num_rows, column, num_columns = part
    wide = math.gcd(column, num_columns) or num_columns
    block = (ROWS, wide * COLUMNS)
    first = earlier is None
    return pl.pallas_call(
        add_kernel,
        grid=(num_rows, num_columns // wide),
        in_specs=[
            pl.BlockSpec(block, lambda i, j: (i + row, j + column // wide)),
            pl.BlockSpec(block, lambda i, j: (i, j)),
        ]
        + ([] if first else [pl.BlockSpec(memory_space=pl.ANY)]),
        out_specs=pl.BlockSpec((1,) + block, lambda i, j: (0, i + row, j + column // wide)),
        out_shape=jax.ShapeDtypeStruct((1, width, depth), BF16),
        input_output_aliases={} if first else {2: 0},
        compiler_params=params(),
        cost_estimate=cost(other.size, other.size * 6),
        name="add_part",
    )(own, other, *(() if first else (earlier,)))


def partial_kernel(counts, head_ref, *refs):
    flat = [c for group in counts for c in group]
    num = len(flat)
    lows, rest, outs = refs[:num], refs[num : -len(counts)], refs[-len(counts) :]
    low = jnp.concatenate([r[...] for r in lows], axis=0)
    sums = jnp.dot(low, head_ref[0], preferred_element_type=F32)
    half = lows[0].shape[0]
    job, at = 0, 0
    for out, group in zip(outs, counts):
        for n, count in enumerate(group):
            total = sums[job * half : (job + 1) * half].astype(BF16).astype(F32)
            for r in rest[at : at + count]:
                total = total + r[...].astype(F32)
            out[n * half : (n + 1) * half, :] = total.astype(out.dtype)
            job, at = job + 1, at + count


def partials(low, head, groups, dtype=BF16):
    _, width, depth = head.shape
    half = low.shape[0] // (2 * BLOCKS)
    step = 2048
    jobs = [job for group in groups for job in group]
    counts = [[len(add) for _, add in group] for group in groups]
    added = [x for _, add in jobs for x in add]
    return pl.pallas_call(
        functools.partial(partial_kernel, counts),
        grid=(depth // step,),
        in_specs=[pl.BlockSpec((1, width, step), lambda i: (0, 0, i))]
        + [pl.BlockSpec((half, width), lambda i, at=at: (at, 0)) for at, _ in jobs]
        + [pl.BlockSpec((half, step), lambda i, row=row: (row, i)) for _, row in added],
        out_specs=[pl.BlockSpec((len(g) * half, step), lambda i: (0, i)) for g in groups],
        out_shape=[jax.ShapeDtypeStruct((len(g) * half, depth), dtype) for g in groups],
        compiler_params=params(),
        cost_estimate=cost(
            2 * len(jobs) * half * width * depth,
            width * depth * 2 + (len(jobs) + len(added)) * half * depth * 2,
        ),
        name="partials",
    )(head, *([low] * len(jobs)), *[x for x, _ in added])


def ring_perm(step):
    return [
        (y * SIDES + s, ((y + step) % RING) * SIDES + s)
        for y in range(RING)
        for s in range(SIDES)
    ]


def gate(values, *needed):
    found = lax.optimization_barrier((tuple(values), tuple(needed)))[0]
    return found if len(found) > 1 else found[0]


def body(hidden, gain, head, teacher_index, teacher_logits, cotangent):
    up, down, across = ring_perm(1), ring_perm(-1), ring_perm(2)
    swap = [(f, f ^ 1) for f in range(BLOCKS)]
    num_pipe = lax.axis_size("pipe")
    mirror = [(p, num_pipe - 1 - p) for p in range(num_pipe)]
    facing = [
        (p * BLOCKS + f, (num_pipe - 1 - p) * BLOCKS + (f ^ 1))
        for p in range(num_pipe)
        for f in range(BLOCKS)
    ]

    def send(x, perm):
        return lax.ppermute(x, "fsdp", perm)

    def exchange(x):
        return lax.ppermute(x, ("pipe", "fsdp"), facing)

    _, width, depth = head.shape
    rows = teacher_index.shape[0]
    tokens = rows // BLOCKS
    num_top = teacher_index.shape[1]
    rest = math.log(smoothing / (width * BLOCKS - num_top))

    a, b = {}, {}
    a[0], scale_a = norm_half(hidden, gain, 0)
    b[0], scale_b = norm_half(hidden, gain, 1)
    a[3] = send(a[0], up)
    a[1] = send(a[0], down)
    a[4] = send(a[0], swap)
    b[3] = send(b[0], up)
    b[1] = send(b[0], down)

    me = lax.axis_index("fsdp")
    slots = jnp.arange(BLOCKS, dtype=jnp.int32)
    order = ((me // SIDES + slots % RING) % RING) * SIDES + (me % SIDES) ^ (slots // RING)
    order = order.astype(jnp.int32)
    base = (me * width).astype(jnp.int32).reshape(1)
    index_t, logits_t = teacher_index.T, teacher_logits.T
    weights = [teacher_weights(order[:RING], base, index_t, logits_t, width, rest)]
    cot = jnp.take(cotangent.reshape(BLOCKS, tokens), order, axis=0)

    groups = ((0,), (3, 1, 4), (5,), (2, 7), (6,))
    b0, a4 = gate((b[0], a[4]), a[3], a[1], weights[0])
    b[4] = send(b0, swap)
    a[7] = send(a4, up)
    a[5] = send(a4, down)
    order, base = gate((order, base), weights[0])
    weights.append(teacher_weights(order[RING:], base, index_t, logits_t, width, rest))
    found = [block_logits(groups[0], a, b, head, weights)]
    a3, b1, b[4] = gate((a[3], b[1], b[4]), b[3], weights[1], found[0][1])
    a[2] = send(a3, up)
    b[2] = send(b1, down)
    b[5] = send(b1, swap)
    found.append(block_logits(groups[1], a, b, head, weights))
    b3, a7, b5 = gate((b[3], a[7], b[5]), a[5], found[1][1])
    b[7] = send(b3, swap)
    a[6] = send(a7, up)
    b[6] = send(b5, down)
    found.append(block_logits(groups[2], a, b, head, weights))
    a[2], b[2], b[7] = gate((a[2], b[2], b[7]), found[2][1])
    found.append(block_logits(groups[3], a, b, head, weights))
    a[6], b[6] = gate((a[6], b[6]), found[3][1])
    found.append(block_logits(groups[4], a, b, head, weights))

    at = [s for group in groups for s in group]
    sums = jnp.concatenate([f[1] for f in found], axis=0)
    sums = jnp.stack([sums[at.index(s)] for s in range(BLOCKS)])

    def rows_of(x):
        return x[:, 0:1], x[:, 1:2], x[:, 2:3]

    other = send(sums, swap)
    other = jnp.concatenate([other[RING:], other[:RING]], axis=0)
    pair = merge_sums([rows_of(sums), rows_of(other)])
    pair = jnp.concatenate(pair + (jnp.zeros((BLOCKS, 5, tokens), F32),), axis=1)
    ring_sums = [pair, send(pair, down), send(pair, across), send(pair, up)]
    first, second, low, loss = all_dlogits(
        groups, [f[0] for f in found], weights, cot, ring_sums, rest
    )

    pieces, facing_pieces = [], []
    for slot in range(BLOCKS):
        pieces += [a[slot], b[slot]]
        other_slot = (slot + RING) % BLOCKS
        facing_pieces += [a[other_slot], b[other_slot]]

    their_first = send(first, swap)
    o2a, o2b = partials(low, head, [[(12, [])], [(13, [])]])
    r_o2a, r_o2b = send(o2a, down), send(o2b, up)

    def part_of(n, mine):
        _, _, column, num_columns = PARTS[n]
        return table_part(mine, facing_pieces, column * COLUMNS, num_columns * COLUMNS)

    their_first, second_there = gate((their_first, second), o2a)
    their_second = send(second_there, swap)
    parts = [part_of(0, their_first), part_of(1, their_first)]
    theirs = [exchange(parts[0]), exchange(parts[1])]
    parts.append(part_of(2, their_second))

    low, first, second, their_first, their_second = gate(
        (low, first, second, their_first, their_second),
        r_o2a, r_o2b, theirs[0], parts[2],
    )
    theirs.append(exchange(parts[2]))
    to_down, to_up, to_swap = partials(
        low,
        head,
        [
            [(14, [(r_o2a, 0)]), (4, [])],
            [(10, []), (5, [])],
            [(11, [(r_o2b, 0)]), (15, [])],
        ],
    )
    o3a_s2a, o1a_s2b, o1b_o3b = send(to_down, down), send(to_up, up), send(to_swap, swap)
    their_first, their_second, first, second = gate(
        (their_first, their_second, first, second), to_down
    )
    own, along = own_table(first, second, head, gain, pieces)
    along = along[:1].reshape(8, depth // 8)
    parts += [part_of(n, their_first if PARTS[n][0] == 0 else their_second) for n in (3, 4, 5)]

    low, own, along, theirs[2], parts[3], parts[4], parts[5] = gate(
        (low, own, along, theirs[2], *parts[3:]), o3a_s2a, o1a_s2b, o1b_o3b, theirs[1]
    )
    theirs.append(exchange(parts[3]))
    along = along + send(along, swap)
    to_down, to_up, to_swap = gate(
        partials(
            low,
            head,
            [
                [(6, [(o3a_s2a, 1)]), (7, [(o1b_o3b, 1)])],
                [(2, []), (3, [(o1a_s2b, 1), (o1b_o3b, 0)])],
                [(8, [(o3a_s2a, 0), (o1a_s2b, 0)]), (9, [])],
            ],
        ),
        along,
    )
    s3, s1, o0 = send(to_down, down), send(to_up, up), send(to_swap, swap)
    merged = None
    for n in range(2):
        merged = add_part(own, theirs[n], merged, PARTS[n])
    merged = add_part(own, theirs[2], merged, PARTS[2])

    low, along, theirs[3], merged = gate((low, along, theirs[3], merged), s3, s1, o0)
    theirs += [exchange(parts[4]), exchange(parts[5])]
    along = along + send(along, [(f, f ^ SIDES) for f in range(BLOCKS)])
    (dnormed,) = partials(
        low, head, [[(n, [(s3, n), (s1, n), (o0, n)]) for n in (0, 1)]], F32
    )
    opposite = [
        (p * BLOCKS + f, (num_pipe - 1 - p) * BLOCKS + t)
        for p in range(num_pipe)
        for f, t in across
    ]
    ours = (along + send(along, across)).astype(BF16)
    mirrored = lax.ppermute(along, "pipe", mirror) + lax.ppermute(
        along, ("pipe", "fsdp"), opposite
    )
    merged_gain = (ours.astype(F32) + mirrored.astype(BF16).astype(F32)).astype(BF16)
    merged_gain = merged_gain.reshape(1, depth)
    scale = jnp.concatenate([scale_a, scale_b], axis=0)[:, :1]
    unit = hidden.astype(F32) * scale
    scaled = gain * dnormed
    grad_states = scale * scaled - scale * unit * jnp.mean(unit * scaled, axis=1, keepdims=True)
    grad_states = grad_states.astype(BF16)
    merged = add_part(own, theirs[3], merged, PARTS[3])

    theirs[4], theirs[5], merged = gate(
        (theirs[4], theirs[5], merged), grad_states, merged_gain
    )
    for n in (4, 5):
        merged = add_part(own, theirs[n], merged, PARTS[n])
    return (loss[0], grad_states, merged, merged_gain)


def solution(mesh):
    in_specs = (
        P(("pipe", "fsdp"), None),
        P("pipe", None),
        P("pipe", "fsdp", None),
        P("pipe", None),
        P("pipe", None),
        P("pipe"),
    )
    out_specs = (
        P(("pipe", "fsdp")),
        P(("pipe", "fsdp"), None),
        P("pipe", "fsdp", None),
        P("pipe", None),
    )
    return jax.shard_map(body, mesh=mesh, in_specs=in_specs, out_specs=out_specs, check_vma=False)
```

```python
import functools
import math

import jax
import jax.numpy as jnp
from jax import lax
from jax.experimental import pallas as pl
from jax.experimental.pallas import tpu as pltpu
from jax.sharding import PartitionSpec as P

smoothing = 0.1
epsilon = 1e-05
F32 = jnp.float32
BF16 = jnp.bfloat16
BIG = 63 * 1024 * 1024

RING, SIDES = 4, 2
BLOCKS = RING * SIDES
ROWS, COLUMNS = 128, 768
PARTS = (
    (0, 1, 3, 5),
    (1, 3, 0, 3),
    (1, 3, 3, 3),
    (1, 3, 6, 2),
    (0, 1, 0, 3),
)


def params(**kw):
    return pltpu.CompilerParams(vmem_limit_bytes=BIG, **kw)


def cost(flops, nbytes):
    del flops, nbytes
    return pl.CostEstimate(flops=1, bytes_accessed=1, transcendentals=0)


def norm_kernel(hidden_ref, gain_ref, normed_ref, scale_ref):
    floats = hidden_ref[...].astype(F32)
    scale = lax.rsqrt(jnp.mean(floats * floats, axis=1, keepdims=True) + epsilon)
    normed_ref[...] = (floats * scale * gain_ref[...]).astype(BF16)
    scale_ref[...] = jnp.broadcast_to(scale, scale_ref.shape)


def norm_half(hidden, gain, half):
    rows, width = hidden.shape
    step = rows // 4
    return pl.pallas_call(
        norm_kernel,
        grid=(2,),
        in_specs=[
            pl.BlockSpec((step, width), lambda i: (i + 2 * half, 0)),
            pl.BlockSpec((1, width), lambda i: (0, 0)),
        ],
        out_specs=[
            pl.BlockSpec((step, width), lambda i: (i, 0)),
            pl.BlockSpec((step, 128), lambda i: (i, 0)),
        ],
        out_shape=[
            jax.ShapeDtypeStruct((rows // 2, width), BF16),
            jax.ShapeDtypeStruct((rows // 2, 128), F32),
        ],
        compiler_params=params(),
        cost_estimate=cost(rows * width * 2, rows * width * 2),
        name="norm_half",
    )(hidden, gain)


def teacher_kernel(rest, order_ref, base_ref, index_ref, logit_ref, out_ref):
    logits = logit_ref[...]
    top = jnp.max(logits, axis=0, keepdims=True)
    shifted = logits - top
    logsum = jnp.log(jnp.sum(jnp.exp(shifted), axis=0, keepdims=True))
    value = rest - (math.log(1.0 - smoothing) + (shifted - logsum))
    entry = index_ref[...] - base_ref[0]
    num_top, tokens = value.shape
    part = 64
    for lower in range(0, out_ref.shape[1], part):
        row = lax.broadcasted_iota(jnp.int32, (part, tokens), 0) + lower
        dense = jnp.zeros((part, tokens), F32)
        for k in range(num_top):
            dense = jnp.where(row == entry[k : k + 1, :], value[k : k + 1, :], dense)
        out_ref[0, lower : lower + part, :] = dense


def teacher_weights(order, base, index, logits, width, rest):
    num_top = index.shape[0]
    slots = order.shape[0]
    tokens = index.shape[1] // BLOCKS
    spec = pl.BlockSpec((num_top, tokens), lambda j, order, base: (0, order[j]))
    return pl.pallas_call(
        functools.partial(teacher_kernel, rest),
        grid_spec=pltpu.PrefetchScalarGridSpec(
            num_scalar_prefetch=2,
            grid=(slots,),
            in_specs=[spec, spec],
            out_specs=pl.BlockSpec((1, width, tokens), lambda j, order, base: (j, 0, 0)),
        ),
        out_shape=jax.ShapeDtypeStruct((slots, width, tokens), F32),
        compiler_params=params(),
        cost_estimate=cost(slots * tokens * width * num_top, slots * tokens * width * 4),
        name="teacher_weights",
    )(order, base, index, logits)


def logits_kernel(count, head_ref, *refs):
    pieces, weights = refs[: 2 * count], refs[2 * count : 3 * count]
    logits_ref, sums_ref = refs[3 * count :]
    step = pl.program_id(0)
    block = jnp.concatenate([p[...] for p in pieces], axis=0)
    part = lax.dot_general(
        head_ref[0], block, (((1,), (1,)), ((), ())), preferred_element_type=F32
    )
    tokens = logits_ref.shape[2]

    @pl.when(step == 0)
    def _():
        for n in range(count):
            logits_ref[n] = part[:, n * tokens : (n + 1) * tokens]

    @pl.when(step > 0)
    def _():
        for n in range(count):
            logits_ref[n] += part[:, n * tokens : (n + 1) * tokens]

    @pl.when(step == pl.num_programs(0) - 1)
    def _():
        for n in range(count):
            logits = logits_ref[n]
            top = jnp.max(logits, axis=0, keepdims=True)
            shifted = logits - top
            expo = jnp.exp(shifted)
            total = jnp.sum(expo, axis=0, keepdims=True)
            mixed = jnp.sum(expo * (shifted + weights[n][0]), axis=0, keepdims=True)
            sums_ref[n] = jnp.concatenate(
                [top, total, mixed, jnp.zeros((5, top.shape[1]), F32)], axis=0
            )


def block_logits(slots, a, b, head, weights):
    _, width, depth = head.shape
    half = a[slots[0]].shape[0]
    tokens = 2 * half
    count = len(slots)
    step = 3072
    return pl.pallas_call(
        functools.partial(logits_kernel, count),
        grid=(depth // step,),
        in_specs=[pl.BlockSpec((1, width, step), lambda i: (0, 0, i))]
        + [pl.BlockSpec((half, step), lambda i: (0, i))] * (2 * count)
        + [pl.BlockSpec((1, width, tokens), lambda i, s=s: (s % RING, 0, 0)) for s in slots],
        out_specs=[
            pl.BlockSpec((count, width, tokens), lambda i: (0, 0, 0)),
            pl.BlockSpec((count, 8, tokens), lambda i: (0, 0, 0)),
        ],
        out_shape=[
            jax.ShapeDtypeStruct((count, width, tokens), F32),
            jax.ShapeDtypeStruct((count, 8, tokens), F32),
        ],
        compiler_params=params(),
        cost_estimate=cost(2 * count * tokens * width * depth, width * depth * 2),
        name="block_logits",
    )(head, *[x[s] for s in slots for x in (a, b)], *[weights[s // RING] for s in slots])


def merge_sums(parts):
    top = functools.reduce(jnp.maximum, [p[0] for p in parts])
    total, mixed = 0.0, 0.0
    for one_top, one_total, one_mixed in parts:
        down = jnp.exp(one_top - top)
        total = total + one_total * down
        mixed = mixed + down * (one_mixed + (one_top - top) * one_total)
    return top, total, mixed


def dlogits_kernel(rest, where, cot_ref, *refs):
    weights, sums = refs[:SIDES], refs[SIDES : SIDES + RING]
    logits = refs[SIDES + RING : -3]
    low_t_ref, low_ref, loss_ref = refs[-3:]
    tokens = cot_ref.shape[1]
    for slot in range(BLOCKS):
        side, ahead = slot // RING, slot % RING
        parts = []
        for shift in range(RING):
            found = sums[shift][side * RING + (ahead + RING - shift) % RING]
            parts.append((found[0:1], found[1:2], found[2:3]))
        top, total, mixed = merge_sums(parts)
        logtotal = jnp.log(total)
        logz = top + logtotal
        loss = mixed / total - logtotal - rest
        group, at = where[slot]
        rel = logits[group][at] - logz
        grads = cot_ref[slot : slot + 1] * jnp.exp(rel) * (
            rel - (rest + loss) + weights[side][ahead]
        )
        here = slice(slot * tokens, (slot + 1) * tokens)
        low_t_ref[:, here] = grads.astype(BF16)
        low_ref[here, :] = jnp.transpose(grads).astype(BF16)
        loss_ref[slot : slot + 1, :] = loss


def some_dlogits(lower, rows, groups, found, weights, cot, sums, rest):
    _, width, tokens = weights[0].shape
    where = {s: (g, n) for g, group in enumerate(groups) for n, s in enumerate(group)}
    step = math.gcd(lower, rows)
    at = lower // step

    def whole(x):
        return pl.BlockSpec(x.shape, lambda i: (0,) * x.ndim)

    def some(x):
        return pl.BlockSpec((x.shape[0], step, tokens), lambda i: (0, i + at, 0))

    return pl.pallas_call(
        functools.partial(dlogits_kernel, rest, where),
        grid=(rows // step,),
        in_specs=[whole(cot)]
        + [some(x) for x in weights]
        + [whole(x) for x in sums]
        + [some(x) for x in found],
        out_specs=[
            pl.BlockSpec((step, BLOCKS * tokens), lambda i: (i, 0)),
            pl.BlockSpec((BLOCKS * tokens, step), lambda i: (0, i)),
            pl.BlockSpec((BLOCKS, tokens), lambda i: (0, 0)),
        ],
        out_shape=[
            jax.ShapeDtypeStruct((rows, BLOCKS * tokens), BF16),
            jax.ShapeDtypeStruct((BLOCKS * tokens, rows), BF16),
            jax.ShapeDtypeStruct((BLOCKS, tokens), F32),
        ],
        compiler_params=params(),
        cost_estimate=cost(0, 0),
        name="some_dlogits",
    )(cot, *weights, *sums, *found)


def part_kernel(low_ref, *refs):
    normed = jnp.concatenate([p[...] for p in refs[:-1]], axis=0)
    refs[-1][...] = jnp.dot(low_ref[...], normed, preferred_element_type=F32).astype(BF16)


def table_part(low_t, pieces, lower, size):
    rows, tokens = low_t.shape
    half = pieces[0].shape[0]
    step = COLUMNS
    start = lower // step
    return pl.pallas_call(
        part_kernel,
        grid=(size // step,),
        in_specs=[pl.BlockSpec((rows, tokens), lambda i: (0, 0))]
        + [pl.BlockSpec((half, step), lambda i: (0, i + start)) for _ in pieces],
        out_specs=pl.BlockSpec((rows, step), lambda i: (0, i)),
        out_shape=jax.ShapeDtypeStruct((rows, size), BF16),
        compiler_params=params(),
        cost_estimate=cost(2 * rows * tokens * size, (rows + tokens) * size * 2),
        name="table_part",
    )(low_t, *pieces)


def table_kernel(first_ref, other_ref, head_ref, gain_ref, *refs):
    pieces, (out_ref, gain_out_ref) = refs[:-2], refs[-2:]
    normed = jnp.concatenate([p[...] for p in pieces], axis=0)
    low = jnp.concatenate([first_ref[...], other_ref[...]], axis=0)
    grads = jnp.dot(low, normed, preferred_element_type=F32)
    out_ref[...] = grads.astype(BF16)
    along = jnp.sum(head_ref[0].astype(F32) * grads, axis=0, keepdims=True) / gain_ref[...]
    gain_out_ref[...] = jnp.broadcast_to(along, gain_out_ref.shape)


def own_table(first, other, head, gain, pieces):
    _, width, depth = head.shape
    tokens = first.shape[1]
    half = pieces[0].shape[0]
    step = COLUMNS
    return pl.pallas_call(
        table_kernel,
        grid=(depth // step,),
        in_specs=[
            pl.BlockSpec(first.shape, lambda i: (0, 0)),
            pl.BlockSpec(other.shape, lambda i: (0, 0)),
            pl.BlockSpec((1, width, step), lambda i: (0, 0, i)),
            pl.BlockSpec((1, step), lambda i: (0, i)),
        ]
        + [pl.BlockSpec((half, step), lambda i: (0, i)) for _ in pieces],
        out_specs=[
            pl.BlockSpec((width, step), lambda i: (0, i)),
            pl.BlockSpec((8, step), lambda i: (0, i)),
        ],
        out_shape=[
            jax.ShapeDtypeStruct((width, depth), BF16),
            jax.ShapeDtypeStruct((8, depth), F32),
        ],
        compiler_params=params(),
        cost_estimate=cost(2 * width * tokens * depth, (tokens + 2 * width) * depth * 2),
        name="own_table",
    )(first, other, head, gain, *pieces)


def add_kernel(own_ref, other_ref, *refs):
    refs[-1][0] = (own_ref[...].astype(F32) + other_ref[...].astype(F32)).astype(BF16)


def add_part(own, other, earlier, part):
    width, depth = own.shape
    row, num_rows, column, num_columns = part
    wide = math.gcd(column, num_columns) or num_columns
    block = (ROWS, wide * COLUMNS)
    first = earlier is None
    return pl.pallas_call(
        add_kernel,
        grid=(num_rows, num_columns // wide),
        in_specs=[
            pl.BlockSpec(block, lambda i, j: (i + row, j + column // wide)),
            pl.BlockSpec(block, lambda i, j: (i, j)),
        ]
        + ([] if first else [pl.BlockSpec(memory_space=pl.ANY)]),
        out_specs=pl.BlockSpec((1,) + block, lambda i, j: (0, i + row, j + column // wide)),
        out_shape=jax.ShapeDtypeStruct((1, width, depth), BF16),
        input_output_aliases={} if first else {2: 0},
        compiler_params=params(),
        cost_estimate=cost(other.size, other.size * 6),
        name="add_part",
    )(own, other, *(() if first else (earlier,)))


def partial_kernel(counts, head_ref, *refs):
    flat = [c for group in counts for c in group]
    num = len(flat)
    lows, rest, outs = refs[: 2 * num], refs[2 * num : -len(counts)], refs[-len(counts) :]
    half = lows[0].shape[0]
    low = jnp.concatenate(
        [jnp.concatenate([r[...] for r in lows[n::num]], axis=1) for n in range(num)], axis=0
    )
    sums = jnp.dot(low, head_ref[0], preferred_element_type=F32)
    job, at = 0, 0
    for out, group in zip(outs, counts):
        for n, count in enumerate(group):
            total = sums[job * half : (job + 1) * half].astype(BF16).astype(F32)
            for r in rest[at : at + count]:
                total = total + r[...].astype(F32)
            out[n * half : (n + 1) * half, :] = total.astype(out.dtype)
            job, at = job + 1, at + count


def partials(low, head, groups, dtype=BF16):
    _, width, depth = head.shape
    half = low[0].shape[0] // (2 * BLOCKS)
    step = 2048
    jobs = [job for group in groups for job in group]
    counts = [[len(add) for _, add in group] for group in groups]
    added = [x for _, add in jobs for x in add]
    return pl.pallas_call(
        functools.partial(partial_kernel, counts),
        grid=(depth // step,),
        in_specs=[pl.BlockSpec((1, width, step), lambda i: (0, 0, i))]
        + [pl.BlockSpec((half, x.shape[1]), lambda i, at=at: (at, 0)) for x in low for at, _ in jobs]
        + [pl.BlockSpec((half, step), lambda i, row=row: (row, i)) for _, row in added],
        out_specs=[pl.BlockSpec((len(g) * half, step), lambda i: (0, i)) for g in groups],
        out_shape=[jax.ShapeDtypeStruct((len(g) * half, depth), dtype) for g in groups],
        compiler_params=params(),
        cost_estimate=cost(
            2 * len(jobs) * half * width * depth,
            width * depth * 2 + (len(jobs) + len(added)) * half * depth * 2,
        ),
        name="partials",
    )(head, *[x for x in low for _ in jobs], *[x for x, _ in added])


def join_kernel(counts, *refs):
    given, outs = refs[: -len(counts)], refs[-len(counts) :]
    sums, rest = given[: len(counts)], given[len(counts) :]
    at = 0
    for out, own, group in zip(outs, sums, counts):
        half = out.shape[0] // len(group)
        for n, count in enumerate(group):
            here = slice(n * half, (n + 1) * half)
            total = own[here, :].astype(F32)
            for r in rest[at : at + count]:
                total = total + r[...].astype(F32)
            at += count
            out[here, :] = total.astype(out.dtype)


def join(own, groups):
    rows, depth = own[0].shape
    step = depth // 2
    counts = [[len(add) for add in group] for group in groups]
    added = [x for group in groups for add in group for x in add]
    whole = pl.BlockSpec((rows, step), lambda i: (0, i))
    return pl.pallas_call(
        functools.partial(join_kernel, counts),
        grid=(depth // step,),
        in_specs=[whole] * len(own)
        + [pl.BlockSpec((rows // 2, step), lambda i, row=row: (row, i)) for _, row in added],
        out_specs=[whole] * len(own),
        out_shape=[jax.ShapeDtypeStruct(x.shape, x.dtype) for x in own],
        compiler_params=params(),
        cost_estimate=cost(0, 0),
        name="join",
    )(*own, *[x for x, _ in added])


def states_kernel(hidden_ref, scale_ref, gain_ref, *refs):
    parts, out_ref = refs[:-1], refs[-1]
    dnormed = parts[0][...].astype(F32)
    for r in parts[1:]:
        dnormed = dnormed + r[...].astype(F32)
    scale = scale_ref[:, 0:1]
    unit = hidden_ref[...].astype(F32) * scale
    scaled = gain_ref[...] * dnormed
    along = jnp.mean(unit * scaled, axis=1, keepdims=True)
    out_ref[...] = (scale * scaled - scale * unit * along).astype(BF16)


def states_gradient(hidden, scale, gain, parts):
    rows, width = hidden.shape
    step = rows // 4
    block = pl.BlockSpec((step, width), lambda i: (i, 0))
    return pl.pallas_call(
        states_kernel,
        grid=(rows // step,),
        in_specs=[
            block,
            pl.BlockSpec((step, scale.shape[1]), lambda i: (i, 0)),
            pl.BlockSpec((1, width), lambda i: (0, 0)),
        ]
        + [block] * len(parts),
        out_specs=block,
        out_shape=jax.ShapeDtypeStruct((rows, width), BF16),
        compiler_params=params(),
        cost_estimate=cost(0, 0),
        name="states_gradient",
    )(hidden, scale, gain, *parts)


def ring_perm(step):
    return [
        (y * SIDES + s, ((y + step) % RING) * SIDES + s)
        for y in range(RING)
        for s in range(SIDES)
    ]


def gate(values, *needed):
    found = lax.optimization_barrier((tuple(values), tuple(needed)))[0]
    return found if len(found) > 1 else found[0]


def body(hidden, gain, head, teacher_index, teacher_logits, cotangent):
    up, down, across = ring_perm(1), ring_perm(-1), ring_perm(2)
    swap = [(f, f ^ 1) for f in range(BLOCKS)]
    num_pipe = lax.axis_size("pipe")
    mirror = [(p, num_pipe - 1 - p) for p in range(num_pipe)]
    facing = [
        (p * BLOCKS + f, (num_pipe - 1 - p) * BLOCKS + (f ^ 1))
        for p in range(num_pipe)
        for f in range(BLOCKS)
    ]

    def send(x, perm):
        return lax.ppermute(x, "fsdp", perm)

    def exchange(x):
        return lax.ppermute(x, ("pipe", "fsdp"), facing)

    _, width, depth = head.shape
    rows = teacher_index.shape[0]
    tokens = rows // BLOCKS
    num_top = teacher_index.shape[1]
    rest = math.log(smoothing / (width * BLOCKS - num_top))

    a, b = {}, {}
    a[0], scale_a = norm_half(hidden, gain, 0)
    b[0], scale_b = norm_half(hidden, gain, 1)
    a[3] = send(a[0], up)
    a[1] = send(a[0], down)
    a[4] = send(a[0], swap)
    b[3] = send(b[0], up)
    b[1] = send(b[0], down)

    me = lax.axis_index("fsdp")
    slots = jnp.arange(BLOCKS, dtype=jnp.int32)
    order = ((me // SIDES + slots % RING) % RING) * SIDES + (me % SIDES) ^ (slots // RING)
    order = order.astype(jnp.int32)
    base = (me * width).astype(jnp.int32).reshape(1)
    index_t, logits_t = teacher_index.T, teacher_logits.T
    weights = [teacher_weights(order[:RING], base, index_t, logits_t, width, rest)]
    cot = jnp.take(cotangent.reshape(BLOCKS, tokens), order, axis=0)

    groups = ((0,), (3, 1, 4), (5,), (2, 7), (6,))
    b0, a4 = gate((b[0], a[4]), a[3], a[1], weights[0])
    b[4] = send(b0, swap)
    a[7] = send(a4, up)
    a[5] = send(a4, down)
    order, base = gate((order, base), weights[0])
    weights.append(teacher_weights(order[RING:], base, index_t, logits_t, width, rest))
    found = [block_logits(groups[0], a, b, head, weights)]
    a3, b1, b[4] = gate((a[3], b[1], b[4]), b[3], weights[1], found[0][1])
    a[2] = send(a3, up)
    b[2] = send(b1, down)
    b[5] = send(b1, swap)
    found.append(block_logits(groups[1], a, b, head, weights))
    b3, a7, b5 = gate((b[3], a[7], b[5]), a[5], found[1][1])
    b[7] = send(b3, swap)
    a[6] = send(a7, up)
    b[6] = send(b5, down)
    found.append(block_logits(groups[2], a, b, head, weights))
    a[2], b[2], b[7] = gate((a[2], b[2], b[7]), found[2][1])
    found.append(block_logits(groups[3], a, b, head, weights))
    a[6], b[6] = gate((a[6], b[6]), found[3][1])
    found.append(block_logits(groups[4], a, b, head, weights))

    at = [s for group in groups for s in group]
    sums = jnp.concatenate([f[1] for f in found], axis=0)
    sums = jnp.stack([sums[at.index(s)] for s in range(BLOCKS)])

    def rows_of(x):
        return x[:, 0:1], x[:, 1:2], x[:, 2:3]

    other = send(sums, swap)
    other = jnp.concatenate([other[RING:], other[:RING]], axis=0)
    pair = merge_sums([rows_of(sums), rows_of(other)])
    pair = jnp.concatenate(pair + (jnp.zeros((BLOCKS, 5, tokens), F32),), axis=1)
    ring_sums = [pair, send(pair, down), send(pair, across), send(pair, up)]
    given = (groups, [f[0] for f in found], weights, cot)
    first, low_first, loss = some_dlogits(0, ROWS, *given, ring_sums, rest)
    their_first = send(first, swap)
    ring_sums = [gate((ring_sums[0],), first)] + ring_sums[1:]
    second, low_second, _ = some_dlogits(ROWS, width - ROWS, *given, ring_sums, rest)
    low = (low_first, low_second)

    pieces, facing_pieces = [], []
    for slot in range(BLOCKS):
        pieces += [a[slot], b[slot]]
        other_slot = (slot + RING) % BLOCKS
        facing_pieces += [a[other_slot], b[other_slot]]

    def part_of(n, low_t):
        _, _, column, num_columns = PARTS[n]
        return table_part(low_t, facing_pieces, column * COLUMNS, num_columns * COLUMNS)

    their_first, second_there = gate((their_first, second), second)
    their_second = send(second_there, swap)
    parts = [part_of(0, their_first)]
    theirs = [exchange(parts[0])]
    o2a, o2b = partials(gate(low, parts[0]), head, [[(12, [])], [(13, [])]])
    r_o2a, r_o2b = send(o2a, down), send(o2b, up)
    ahead = partials(
        gate(low, o2a),
        head,
        [[(14, []), (4, [])], [(10, []), (5, [])], [(11, []), (15, [])]],
    )
    their_second = gate((their_second,), *ahead)
    parts.append(part_of(1, their_second))

    *low, first, second, their_first, their_second, a0, a1, a2 = gate(
        (*low, first, second, their_first, their_second, *ahead),
        r_o2a, r_o2b, theirs[0], parts[1],
    )
    theirs.append(exchange(parts[1]))
    to_down, to_swap = join([a0, a2], [[[(r_o2a, 0)], []], [[(r_o2b, 0)], []]])
    o3a_s2a, o1a_s2b, o1b_o3b = send(to_down, down), send(a1, up), send(to_swap, swap)
    their_first, their_second = gate((their_first, their_second), to_down)
    parts += [part_of(2, their_second), part_of(3, their_second), part_of(4, their_first)]
    theirs.append(exchange(parts[2]))
    ahead = partials(
        gate(low, to_down), head, [[(6, []), (7, [])], [(2, []), (3, [])], [(8, []), (9, [])]]
    )

    *low, first, second, theirs[1], parts[3], parts[4], a0, a1, a2 = gate(
        (*low, first, second, theirs[1], parts[3], parts[4], *ahead),
        o3a_s2a, o1a_s2b, o1b_o3b,
    )
    theirs.append(exchange(parts[3]))
    to_down, to_up, to_swap = join(
        [a0, a1, a2],
        [
            [[(o3a_s2a, 1)], [(o1b_o3b, 1)]],
            [[], [(o1a_s2b, 1), (o1b_o3b, 0)]],
            [[(o3a_s2a, 0), (o1a_s2b, 0)], []],
        ],
    )
    s3, s1, o0 = send(to_down, down), send(to_up, up), send(to_swap, swap)
    *low, first, second = gate((*low, first, second), to_down)
    own, along = own_table(first, second, head, gain, pieces)
    along = along[:1].reshape(8, depth // 8)
    (mine,) = partials(low, head, [[(0, []), (1, [])]])
    merged = None
    for n in range(2):
        merged = add_part(own, theirs[n], merged, PARTS[n])
    parts[4] = gate((parts[4],), theirs[2], merged)
    theirs.append(exchange(parts[4]))
    merged = add_part(own, theirs[2], merged, PARTS[2])

    mine, along, merged = gate((mine, along, merged), s3, s1, o0)
    along = along + send(along, swap)
    scale = jnp.concatenate([scale_a, scale_b], axis=0)
    grad_states = states_gradient(hidden, scale, gain, [mine, s3, s1, o0])
    merged = add_part(own, theirs[3], merged, PARTS[3])
    along = gate((along,), grad_states)
    along = along + send(along, [(f, f ^ SIDES) for f in range(BLOCKS)])
    along = gate((along,), merged)
    opposite = [
        (p * BLOCKS + f, (num_pipe - 1 - p) * BLOCKS + t)
        for p in range(num_pipe)
        for f, t in across
    ]
    ours = (along + send(along, across)).astype(BF16)
    mirrored = lax.ppermute(along, "pipe", mirror) + lax.ppermute(
        along, ("pipe", "fsdp"), opposite
    )
    merged_gain = (ours.astype(F32) + mirrored.astype(BF16).astype(F32)).astype(BF16)
    merged_gain = merged_gain.reshape(1, depth)
    theirs[4], merged = gate((theirs[4], merged), grad_states)
    merged = add_part(own, theirs[4], merged, PARTS[4])
    return (loss[0], grad_states, merged, merged_gain)


def solution(mesh):
    in_specs = (
        P(("pipe", "fsdp"), None),
        P("pipe", None),
        P("pipe", "fsdp", None),
        P("pipe", None),
        P("pipe", None),
        P("pipe"),
    )
    out_specs = (
        P(("pipe", "fsdp")),
        P(("pipe", "fsdp"), None),
        P("pipe", "fsdp", None),
        P("pipe", None),
    )
    return jax.shard_map(body, mesh=mesh, in_specs=in_specs, out_specs=out_specs, check_vma=False)
```

```python
import functools
import math

import jax
import jax.numpy as jnp
from jax import lax
from jax.experimental import pallas as pl
from jax.experimental.pallas import tpu as pltpu
from jax.sharding import PartitionSpec as P

smoothing = 0.1
epsilon = 1e-05
F32 = jnp.float32
BF16 = jnp.bfloat16
BIG = 63 * 1024 * 1024

RING, SIDES = 4, 2
BLOCKS = RING * SIDES
ROWS, COLUMNS = 128, 768
PARTS = (
    (0, 1, 3, 5),
    (1, 3, 0, 3),
    (1, 3, 3, 3),
    (1, 3, 6, 2),
    (0, 1, 0, 3),
)


def params(**kw):
    return pltpu.CompilerParams(vmem_limit_bytes=BIG, **kw)


def cost(flops, nbytes):
    del flops, nbytes
    return pl.CostEstimate(flops=1, bytes_accessed=1, transcendentals=0)


def norm_kernel(hidden_ref, gain_ref, normed_ref, scale_ref):
    floats = hidden_ref[...].astype(F32)
    scale = lax.rsqrt(jnp.mean(floats * floats, axis=1, keepdims=True) + epsilon)
    normed_ref[...] = (floats * scale * gain_ref[...]).astype(BF16)
    scale_ref[...] = jnp.broadcast_to(scale, scale_ref.shape)


def norm_half(hidden, gain, half):
    rows, width = hidden.shape
    step = rows // 4
    return pl.pallas_call(
        norm_kernel,
        grid=(2,),
        in_specs=[
            pl.BlockSpec((step, width), lambda i: (i + 2 * half, 0)),
            pl.BlockSpec((1, width), lambda i: (0, 0)),
        ],
        out_specs=[
            pl.BlockSpec((step, width), lambda i: (i, 0)),
            pl.BlockSpec((step, 128), lambda i: (i, 0)),
        ],
        out_shape=[
            jax.ShapeDtypeStruct((rows // 2, width), BF16),
            jax.ShapeDtypeStruct((rows // 2, 128), F32),
        ],
        compiler_params=params(),
        cost_estimate=cost(rows * width * 2, rows * width * 2),
        name="norm_half",
    )(hidden, gain)


def teacher_kernel(rest, order_ref, base_ref, index_ref, logit_ref, out_ref):
    logits = logit_ref[...]
    top = jnp.max(logits, axis=0, keepdims=True)
    shifted = logits - top
    logsum = jnp.log(jnp.sum(jnp.exp(shifted), axis=0, keepdims=True))
    value = rest - (math.log(1.0 - smoothing) + (shifted - logsum))
    entry = index_ref[...] - base_ref[0]
    num_top, tokens = value.shape
    part = 64
    for lower in range(0, out_ref.shape[1], part):
        row = lax.broadcasted_iota(jnp.int32, (part, tokens), 0) + lower
        dense = jnp.zeros((part, tokens), F32)
        for k in range(num_top):
            dense = jnp.where(row == entry[k : k + 1, :], value[k : k + 1, :], dense)
        out_ref[0, lower : lower + part, :] = dense


def teacher_weights(order, base, index, logits, width, rest):
    num_top = index.shape[0]
    slots = order.shape[0]
    tokens = index.shape[1] // BLOCKS
    spec = pl.BlockSpec((num_top, tokens), lambda j, order, base: (0, order[j]))
    return pl.pallas_call(
        functools.partial(teacher_kernel, rest),
        grid_spec=pltpu.PrefetchScalarGridSpec(
            num_scalar_prefetch=2,
            grid=(slots,),
            in_specs=[spec, spec],
            out_specs=pl.BlockSpec((1, width, tokens), lambda j, order, base: (j, 0, 0)),
        ),
        out_shape=jax.ShapeDtypeStruct((slots, width, tokens), F32),
        compiler_params=params(),
        cost_estimate=cost(slots * tokens * width * num_top, slots * tokens * width * 4),
        name="teacher_weights",
    )(order, base, index, logits)


def logits_kernel(slots, earlier, head_ref, *refs):
    count = len(slots)
    pieces, weights, before = refs[: 2 * count], refs[2 * count : 3 * count], refs[3 * count : -2]
    logits_ref, sums_ref = refs[-2:]
    step = pl.program_id(0)
    block = jnp.concatenate([p[...] for p in pieces], axis=0)
    part = lax.dot_general(
        head_ref[0], block, (((1,), (1,)), ((), ())), preferred_element_type=F32
    )
    tokens = logits_ref.shape[2]

    @pl.when(step == 0)
    def _():
        for n in range(count):
            logits_ref[n] = part[:, n * tokens : (n + 1) * tokens]

    @pl.when(step > 0)
    def _():
        for n in range(count):
            logits_ref[n] += part[:, n * tokens : (n + 1) * tokens]

    @pl.when(step == pl.num_programs(0) - 1)
    def _():
        for n in range(count):
            logits = logits_ref[n]
            top = jnp.max(logits, axis=0, keepdims=True)
            shifted = logits - top
            expo = jnp.exp(shifted)
            total = jnp.sum(expo, axis=0, keepdims=True)
            mixed = jnp.sum(expo * (shifted + weights[n][0]), axis=0, keepdims=True)
            for at, value in enumerate((top, total, mixed)):
                row = at * BLOCKS + slots[n]
                sums_ref[row : row + 1, :] = value
        for group, ref in zip(earlier, before):
            for slot in group:
                for row in range(slot, 3 * BLOCKS, BLOCKS):
                    sums_ref[row : row + 1, :] = ref[row : row + 1, :]


def block_logits(slots, a, b, head, weights, earlier=(), before=()):
    _, width, depth = head.shape
    half = a[slots[0]].shape[0]
    tokens = 2 * half
    count = len(slots)
    step = 3072
    return pl.pallas_call(
        functools.partial(logits_kernel, slots, earlier),
        grid=(depth // step,),
        in_specs=[pl.BlockSpec((1, width, step), lambda i: (0, 0, i))]
        + [pl.BlockSpec((half, step), lambda i: (0, i))] * (2 * count)
        + [pl.BlockSpec((1, width, tokens), lambda i, s=s: (s % RING, 0, 0)) for s in slots]
        + [pl.BlockSpec((3 * BLOCKS, tokens), lambda i: (0, 0))] * len(before),
        out_specs=[
            pl.BlockSpec((count, width, tokens), lambda i: (0, 0, 0)),
            pl.BlockSpec((3 * BLOCKS, tokens), lambda i: (0, 0)),
        ],
        out_shape=[
            jax.ShapeDtypeStruct((count, width, tokens), F32),
            jax.ShapeDtypeStruct((3 * BLOCKS, tokens), F32),
        ],
        compiler_params=params(),
        cost_estimate=cost(2 * count * tokens * width * depth, width * depth * 2),
        name="block_logits",
    )(head, *[x[s] for s in slots for x in (a, b)], *[weights[s // RING] for s in slots], *before)


def merge_sums(parts):
    top = functools.reduce(jnp.maximum, [p[0] for p in parts])
    total, mixed = 0.0, 0.0
    for one_top, one_total, one_mixed in parts:
        down = jnp.exp(one_top - top)
        total = total + one_total * down
        mixed = mixed + down * (one_mixed + (one_top - top) * one_total)
    return top, total, mixed


def dlogits_kernel(rest, where, cot_ref, *refs):
    weights, sums = refs[:SIDES], refs[SIDES : SIDES + RING]
    logits = refs[SIDES + RING : -3]
    low_t_ref, low_ref, loss_ref = refs[-3:]
    tokens = cot_ref.shape[1]
    parts = []
    for shift in range(RING):
        found = []
        for lower in range(0, 3 * BLOCKS, RING):
            if shift:
                found.append(sums[shift][lower + RING - shift : lower + RING, :])
            found.append(sums[shift][lower : lower + RING - shift, :])
        found = jnp.concatenate(found, axis=0)
        parts.append([found[n * BLOCKS : (n + 1) * BLOCKS] for n in range(3)])
    top, total, mixed = merge_sums(parts)
    logtotals = jnp.log(total)
    logzs = top + logtotals
    losses = mixed / total - logtotals - rest
    loss_ref[...] = losses
    for slot in range(BLOCKS):
        side, ahead = slot // RING, slot % RING
        logz, loss = logzs[slot : slot + 1], losses[slot : slot + 1]
        group, at = where[slot]
        rel = logits[group][at] - logz
        grads = cot_ref[slot : slot + 1] * jnp.exp(rel) * (
            rel - (rest + loss) + weights[side][ahead]
        )
        here = slice(slot * tokens, (slot + 1) * tokens)
        low_t_ref[:, here] = grads.astype(BF16)
        low_ref[here, :] = jnp.transpose(grads).astype(BF16)


def some_dlogits(lower, rows, groups, found, weights, cot, sums, rest):
    _, width, tokens = weights[0].shape
    where = {s: (g, n) for g, group in enumerate(groups) for n, s in enumerate(group)}
    step = math.gcd(lower, rows)
    at = lower // step

    def whole(x):
        return pl.BlockSpec(x.shape, lambda i: (0,) * x.ndim)

    def some(x):
        return pl.BlockSpec((x.shape[0], step, tokens), lambda i: (0, i + at, 0))

    return pl.pallas_call(
        functools.partial(dlogits_kernel, rest, where),
        grid=(rows // step,),
        in_specs=[whole(cot)]
        + [some(x) for x in weights]
        + [whole(x) for x in sums]
        + [some(x) for x in found],
        out_specs=[
            pl.BlockSpec((step, BLOCKS * tokens), lambda i: (i, 0)),
            pl.BlockSpec((BLOCKS * tokens, step), lambda i: (0, i)),
            pl.BlockSpec((BLOCKS, tokens), lambda i: (0, 0)),
        ],
        out_shape=[
            jax.ShapeDtypeStruct((rows, BLOCKS * tokens), BF16),
            jax.ShapeDtypeStruct((BLOCKS * tokens, rows), BF16),
            jax.ShapeDtypeStruct((BLOCKS, tokens), F32),
        ],
        compiler_params=params(),
        cost_estimate=cost(0, 0),
        name="some_dlogits",
    )(cot, *weights, *sums, *found)


def part_kernel(low_ref, *refs):
    normed = jnp.concatenate([p[...] for p in refs[:-1]], axis=0)
    refs[-1][...] = jnp.dot(low_ref[...], normed, preferred_element_type=F32).astype(BF16)


def table_part(low_t, pieces, lower, size):
    rows, tokens = low_t.shape
    half = pieces[0].shape[0]
    step = COLUMNS
    start = lower // step
    return pl.pallas_call(
        part_kernel,
        grid=(size // step,),
        in_specs=[pl.BlockSpec((rows, tokens), lambda i: (0, 0))]
        + [pl.BlockSpec((half, step), lambda i: (0, i + start)) for _ in pieces],
        out_specs=pl.BlockSpec((rows, step), lambda i: (0, i)),
        out_shape=jax.ShapeDtypeStruct((rows, size), BF16),
        compiler_params=params(),
        cost_estimate=cost(2 * rows * tokens * size, (rows + tokens) * size * 2),
        name="table_part",
    )(low_t, *pieces)


def table_kernel(first_ref, other_ref, head_ref, gain_ref, *refs):
    pieces, (out_ref, gain_out_ref) = refs[:-2], refs[-2:]
    normed = jnp.concatenate([p[...] for p in pieces], axis=0)
    low = jnp.concatenate([first_ref[...], other_ref[...]], axis=0)
    grads = jnp.dot(low, normed, preferred_element_type=F32)
    out_ref[...] = grads.astype(BF16)
    along = jnp.sum(head_ref[0].astype(F32) * grads, axis=0, keepdims=True) / gain_ref[...]
    gain_out_ref[...] = jnp.broadcast_to(along, gain_out_ref.shape)


def own_table(first, other, head, gain, pieces):
    _, width, depth = head.shape
    tokens = first.shape[1]
    half = pieces[0].shape[0]
    step = COLUMNS
    return pl.pallas_call(
        table_kernel,
        grid=(depth // step,),
        in_specs=[
            pl.BlockSpec(first.shape, lambda i: (0, 0)),
            pl.BlockSpec(other.shape, lambda i: (0, 0)),
            pl.BlockSpec((1, width, step), lambda i: (0, 0, i)),
            pl.BlockSpec((1, step), lambda i: (0, i)),
        ]
        + [pl.BlockSpec((half, step), lambda i: (0, i)) for _ in pieces],
        out_specs=[
            pl.BlockSpec((width, step), lambda i: (0, i)),
            pl.BlockSpec((8, step), lambda i: (0, i)),
        ],
        out_shape=[
            jax.ShapeDtypeStruct((width, depth), BF16),
            jax.ShapeDtypeStruct((8, depth), F32),
        ],
        compiler_params=params(),
        cost_estimate=cost(2 * width * tokens * depth, (tokens + 2 * width) * depth * 2),
        name="own_table",
    )(first, other, head, gain, *pieces)


def add_kernel(own_ref, other_ref, *refs):
    refs[-1][0] = (own_ref[...].astype(F32) + other_ref[...].astype(F32)).astype(BF16)


def add_part(own, other, earlier, part):
    width, depth = own.shape
    row, num_rows, column, num_columns = part
    wide = math.gcd(column, num_columns) or num_columns
    block = (ROWS, wide * COLUMNS)
    first = earlier is None
    return pl.pallas_call(
        add_kernel,
        grid=(num_rows, num_columns // wide),
        in_specs=[
            pl.BlockSpec(block, lambda i, j: (i + row, j + column // wide)),
            pl.BlockSpec(block, lambda i, j: (i, j)),
        ]
        + ([] if first else [pl.BlockSpec(memory_space=pl.ANY)]),
        out_specs=pl.BlockSpec((1,) + block, lambda i, j: (0, i + row, j + column // wide)),
        out_shape=jax.ShapeDtypeStruct((1, width, depth), BF16),
        input_output_aliases={} if first else {2: 0},
        compiler_params=params(),
        cost_estimate=cost(other.size, other.size * 6),
        name="add_part",
    )(own, other, *(() if first else (earlier,)))


def partial_kernel(counts, head_ref, *refs):
    flat = [c for group in counts for c in group]
    num = len(flat)
    lows, rest, outs = refs[: 2 * num], refs[2 * num : -len(counts)], refs[-len(counts) :]
    half = lows[0].shape[0]
    low = jnp.concatenate(
        [jnp.concatenate([r[...] for r in lows[n::num]], axis=1) for n in range(num)], axis=0
    )
    sums = jnp.dot(low, head_ref[0], preferred_element_type=F32)
    job, at = 0, 0
    for out, group in zip(outs, counts):
        for n, count in enumerate(group):
            total = sums[job * half : (job + 1) * half].astype(BF16).astype(F32)
            for r in rest[at : at + count]:
                total = total + r[...].astype(F32)
            out[n * half : (n + 1) * half, :] = total.astype(out.dtype)
            job, at = job + 1, at + count


def partials(low, head, groups, dtype=BF16):
    _, width, depth = head.shape
    half = low[0].shape[0] // (2 * BLOCKS)
    step = 2048
    jobs = [job for group in groups for job in group]
    counts = [[len(add) for _, add in group] for group in groups]
    added = [x for _, add in jobs for x in add]
    return pl.pallas_call(
        functools.partial(partial_kernel, counts),
        grid=(depth // step,),
        in_specs=[pl.BlockSpec((1, width, step), lambda i: (0, 0, i))]
        + [pl.BlockSpec((half, x.shape[1]), lambda i, at=at: (at, 0)) for x in low for at, _ in jobs]
        + [pl.BlockSpec((half, step), lambda i, row=row: (row, i)) for _, row in added],
        out_specs=[pl.BlockSpec((len(g) * half, step), lambda i: (0, i)) for g in groups],
        out_shape=[jax.ShapeDtypeStruct((len(g) * half, depth), dtype) for g in groups],
        compiler_params=params(),
        cost_estimate=cost(
            2 * len(jobs) * half * width * depth,
            width * depth * 2 + (len(jobs) + len(added)) * half * depth * 2,
        ),
        name="partials",
    )(head, *[x for x in low for _ in jobs], *[x for x, _ in added])


def join_kernel(counts, *refs):
    given, outs = refs[: -len(counts)], refs[-len(counts) :]
    sums, rest = given[: len(counts)], given[len(counts) :]
    at = 0
    for out, own, group in zip(outs, sums, counts):
        half = out.shape[0] // len(group)
        for n, count in enumerate(group):
            here = slice(n * half, (n + 1) * half)
            total = own[here, :].astype(F32)
            for r in rest[at : at + count]:
                total = total + r[...].astype(F32)
            at += count
            out[here, :] = total.astype(out.dtype)


def join(own, groups):
    rows, depth = own[0].shape
    step = depth // 2
    counts = [[len(add) for add in group] for group in groups]
    added = [x for group in groups for add in group for x in add]
    whole = pl.BlockSpec((rows, step), lambda i: (0, i))
    return pl.pallas_call(
        functools.partial(join_kernel, counts),
        grid=(depth // step,),
        in_specs=[whole] * len(own)
        + [pl.BlockSpec((rows // 2, step), lambda i, row=row: (row, i)) for _, row in added],
        out_specs=[whole] * len(own),
        out_shape=[jax.ShapeDtypeStruct(x.shape, x.dtype) for x in own],
        compiler_params=params(),
        cost_estimate=cost(0, 0),
        name="join",
    )(*own, *[x for x, _ in added])


def states_kernel(hidden_ref, scale_ref, gain_ref, *refs):
    parts, out_ref = refs[:-1], refs[-1]
    dnormed = parts[0][...].astype(F32)
    for r in parts[1:]:
        dnormed = dnormed + r[...].astype(F32)
    scale = scale_ref[:, 0:1]
    unit = hidden_ref[...].astype(F32) * scale
    scaled = gain_ref[...] * dnormed
    along = jnp.mean(unit * scaled, axis=1, keepdims=True)
    out_ref[...] = (scale * scaled - scale * unit * along).astype(BF16)


def states_gradient(hidden, scale, gain, parts):
    rows, width = hidden.shape
    step = rows // 4
    block = pl.BlockSpec((step, width), lambda i: (i, 0))
    return pl.pallas_call(
        states_kernel,
        grid=(rows // step,),
        in_specs=[
            block,
            pl.BlockSpec((step, scale.shape[1]), lambda i: (i, 0)),
            pl.BlockSpec((1, width), lambda i: (0, 0)),
        ]
        + [block] * len(parts),
        out_specs=block,
        out_shape=jax.ShapeDtypeStruct((rows, width), BF16),
        compiler_params=params(),
        cost_estimate=cost(0, 0),
        name="states_gradient",
    )(hidden, scale, gain, *parts)


def ring_perm(step):
    return [
        (y * SIDES + s, ((y + step) % RING) * SIDES + s)
        for y in range(RING)
        for s in range(SIDES)
    ]


def gate(values, *needed):
    found = lax.optimization_barrier((tuple(values), tuple(needed)))[0]
    return found if len(found) > 1 else found[0]


def body(hidden, gain, head, teacher_index, teacher_logits, cotangent):
    up, down, across = ring_perm(1), ring_perm(-1), ring_perm(2)
    swap = [(f, f ^ 1) for f in range(BLOCKS)]
    num_pipe = lax.axis_size("pipe")
    mirror = [(p, num_pipe - 1 - p) for p in range(num_pipe)]
    facing = [
        (p * BLOCKS + f, (num_pipe - 1 - p) * BLOCKS + (f ^ 1))
        for p in range(num_pipe)
        for f in range(BLOCKS)
    ]

    def send(x, perm):
        return lax.ppermute(x, "fsdp", perm)

    def exchange(x):
        return lax.ppermute(x, ("pipe", "fsdp"), facing)

    _, width, depth = head.shape
    rows = teacher_index.shape[0]
    tokens = rows // BLOCKS
    num_top = teacher_index.shape[1]
    rest = math.log(smoothing / (width * BLOCKS - num_top))

    a, b = {}, {}
    a[0], scale_a = norm_half(hidden, gain, 0)
    b[0], scale_b = norm_half(hidden, gain, 1)
    a[3] = send(a[0], up)
    a[1] = send(a[0], down)
    a[4] = send(a[0], swap)
    b[3] = send(b[0], up)
    b[1] = send(b[0], down)

    me = lax.axis_index("fsdp")
    slots = jnp.arange(BLOCKS, dtype=jnp.int32)
    order = ((me // SIDES + slots % RING) % RING) * SIDES + (me % SIDES) ^ (slots // RING)
    order = order.astype(jnp.int32)
    base = (me * width).astype(jnp.int32).reshape(1)
    index_t, logits_t = teacher_index.T, teacher_logits.T
    weights = [teacher_weights(order[:RING], base, index_t, logits_t, width, rest)]
    cot = jnp.take(cotangent.reshape(BLOCKS, tokens), order, axis=0)

    groups = ((0,), (3, 1, 4), (5,), (2, 7), (6,))
    b0, a[4] = gate((b[0], a[4]), a[3], a[1], weights[0])
    b[4] = send(b0, swap)
    found = [block_logits(groups[0], a, b, head, weights)]
    a4, order, base = gate((a[4], order, base), found[0][1])
    a[7] = send(a4, up)
    a[5] = send(a4, down)
    weights.append(teacher_weights(order[RING:], base, index_t, logits_t, width, rest))
    a3, b1, b[4] = gate((a[3], b[1], b[4]), b[3])
    a[2] = send(a3, up)
    b[2] = send(b1, down)
    b[5] = send(b1, swap)
    found.append(block_logits(groups[1], a, b, head, weights))
    b3, a7, b5 = gate((b[3], a[7], b[5]), a[5], found[1][1])
    b[7] = send(b3, swap)
    a[6] = send(a7, up)
    b[6] = send(b5, down)
    found.append(block_logits(groups[2], a, b, head, weights))
    a[2], b[2], b[7] = gate((a[2], b[2], b[7]), found[2][1])
    found.append(block_logits(groups[3], a, b, head, weights))
    a[6], b[6] = gate((a[6], b[6]), found[3][1])
    found.append(
        block_logits(groups[4], a, b, head, weights, groups[:4], [f[1] for f in found])
    )
    sums = found[-1][1]
    other = send(sums, swap).reshape(3, SIDES, RING, tokens)[:, ::-1].reshape(sums.shape)
    pair = jnp.concatenate(
        merge_sums([[x[n : n + BLOCKS] for n in range(0, 3 * BLOCKS, BLOCKS)] for x in (sums, other)]),
        axis=0,
    )
    ring_sums = [pair, send(pair, down), send(pair, across), send(pair, up)]
    given = (groups, [f[0] for f in found], weights, cot)
    first, low_first, loss = some_dlogits(0, ROWS, *given, ring_sums, rest)
    their_first = send(first, swap)
    ring_sums = [gate((ring_sums[0],), first)] + ring_sums[1:]
    second, low_second, _ = some_dlogits(ROWS, width - ROWS, *given, ring_sums, rest)
    low = (low_first, low_second)

    pieces, facing_pieces = [], []
    for slot in range(BLOCKS):
        pieces += [a[slot], b[slot]]
        other_slot = (slot + RING) % BLOCKS
        facing_pieces += [a[other_slot], b[other_slot]]

    def part_of(n, low_t):
        _, _, column, num_columns = PARTS[n]
        return table_part(low_t, facing_pieces, column * COLUMNS, num_columns * COLUMNS)

    their_first, second_there = gate((their_first, second), second)
    their_second = send(second_there, swap)
    parts = [part_of(0, their_first)]
    theirs = [exchange(parts[0])]
    o2a, o2b = partials(gate(low, parts[0]), head, [[(12, [])], [(13, [])]])
    r_o2a, r_o2b = send(o2a, down), send(o2b, up)
    ahead = partials(
        gate(low, o2a),
        head,
        [[(14, []), (4, [])], [(10, []), (5, [])], [(11, []), (15, [])]],
    )
    their_second = gate((their_second,), *ahead)
    parts.append(part_of(1, their_second))

    *low, first, second, their_first, their_second, a0, a1, a2 = gate(
        (*low, first, second, their_first, their_second, *ahead),
        r_o2a, r_o2b, theirs[0], parts[1],
    )
    theirs.append(exchange(parts[1]))
    to_down, to_swap = join([a0, a2], [[[(r_o2a, 0)], []], [[(r_o2b, 0)], []]])
    o3a_s2a, o1a_s2b, o1b_o3b = send(to_down, down), send(a1, up), send(to_swap, swap)
    their_first, their_second = gate((their_first, their_second), to_down)
    parts += [part_of(2, their_second), part_of(3, their_second), part_of(4, their_first)]
    theirs.append(exchange(parts[2]))
    ahead = partials(
        gate(low, to_down), head, [[(6, []), (7, [])], [(2, []), (3, [])], [(8, []), (9, [])]]
    )

    *low, first, second, theirs[1], parts[3], parts[4], a0, a1, a2 = gate(
        (*low, first, second, theirs[1], parts[3], parts[4], *ahead),
        o3a_s2a, o1a_s2b, o1b_o3b,
    )
    theirs.append(exchange(parts[3]))
    to_down, to_up, to_swap = join(
        [a0, a1, a2],
        [
            [[(o3a_s2a, 1)], [(o1b_o3b, 1)]],
            [[], [(o1a_s2b, 1), (o1b_o3b, 0)]],
            [[(o3a_s2a, 0), (o1a_s2b, 0)], []],
        ],
    )
    s3, s1, o0 = send(to_down, down), send(to_up, up), send(to_swap, swap)
    *low, first, second = gate((*low, first, second), to_down)
    own, along = own_table(first, second, head, gain, pieces)
    along = along[:1].reshape(8, depth // 8)
    (mine,) = partials(low, head, [[(0, []), (1, [])]])
    merged = None
    for n in range(2):
        merged = add_part(own, theirs[n], merged, PARTS[n])
    parts[4] = gate((parts[4],), theirs[2], merged)
    theirs.append(exchange(parts[4]))
    merged = add_part(own, theirs[2], merged, PARTS[2])

    mine, along, merged = gate((mine, along, merged), s3, s1, o0)
    along = along + send(along, swap)
    scale = jnp.concatenate([scale_a, scale_b], axis=0)
    grad_states = states_gradient(hidden, scale, gain, [mine, s3, s1, o0])
    merged = add_part(own, theirs[3], merged, PARTS[3])
    along = gate((along,), grad_states)
    along = along + send(along, [(f, f ^ SIDES) for f in range(BLOCKS)])
    along = gate((along,), merged)
    opposite = [
        (p * BLOCKS + f, (num_pipe - 1 - p) * BLOCKS + t)
        for p in range(num_pipe)
        for f, t in across
    ]
    ours = (along + send(along, across)).astype(BF16)
    mirrored = lax.ppermute(along, "pipe", mirror) + lax.ppermute(
        along, ("pipe", "fsdp"), opposite
    )
    merged_gain = (ours.astype(F32) + mirrored.astype(BF16).astype(F32)).astype(BF16)
    merged_gain = merged_gain.reshape(1, depth)
    theirs[4], merged = gate((theirs[4], merged), grad_states)
    merged = add_part(own, theirs[4], merged, PARTS[4])
    return (loss[0], grad_states, merged, merged_gain)


def solution(mesh):
    in_specs = (
        P(("pipe", "fsdp"), None),
        P("pipe", None),
        P("pipe", "fsdp", None),
        P("pipe", None),
        P("pipe", None),
        P("pipe"),
    )
    out_specs = (
        P(("pipe", "fsdp")),
        P(("pipe", "fsdp"), None),
        P("pipe", "fsdp", None),
        P("pipe", None),
    )
    return jax.shard_map(body, mesh=mesh, in_specs=in_specs, out_specs=out_specs, check_vma=False)
```

```python
import functools
import math

import jax
import jax.numpy as jnp
from jax import lax
from jax.experimental import pallas as pl
from jax.experimental.pallas import tpu as pltpu
from jax.sharding import PartitionSpec as P

smoothing = 0.1
epsilon = 1e-05
F32 = jnp.float32
BF16 = jnp.bfloat16
BIG = 65408 * 1024

RING, SIDES = 4, 2
BLOCKS = RING * SIDES
ROWS, COLUMNS = 128, 768
PARTS = (
    (0, 1, 2, 6),
    (1, 3, 0, 3),
    (1, 3, 3, 3),
    (1, 3, 6, 2),
    (0, 1, 0, 2),
)


def params(**kw):
    return pltpu.CompilerParams(vmem_limit_bytes=BIG, **kw)


def cost(flops, nbytes):
    del flops, nbytes
    return pl.CostEstimate(flops=1, bytes_accessed=1, transcendentals=0)


def norm_kernel(hidden_ref, gain_ref, normed_ref, scale_ref):
    floats = hidden_ref[...].astype(F32)
    scale = lax.rsqrt(jnp.mean(floats * floats, axis=1, keepdims=True) + epsilon)
    normed_ref[...] = (floats * scale * gain_ref[...]).astype(BF16)
    scale_ref[...] = jnp.broadcast_to(scale, scale_ref.shape)


def norm_half(hidden, gain, half):
    rows, width = hidden.shape
    step = rows // 4
    return pl.pallas_call(
        norm_kernel,
        grid=(2,),
        in_specs=[
            pl.BlockSpec((step, width), lambda i: (i + 2 * half, 0)),
            pl.BlockSpec((1, width), lambda i: (0, 0)),
        ],
        out_specs=[
            pl.BlockSpec((step, width), lambda i: (i, 0)),
            pl.BlockSpec((step, 128), lambda i: (i, 0)),
        ],
        out_shape=[
            jax.ShapeDtypeStruct((rows // 2, width), BF16),
            jax.ShapeDtypeStruct((rows // 2, 128), F32),
        ],
        compiler_params=params(),
        cost_estimate=cost(rows * width * 2, rows * width * 2),
        name="norm_half",
    )(hidden, gain)


def teacher_kernel(rest, order_ref, base_ref, index_ref, logit_ref, out_ref):
    logits = logit_ref[...]
    top = jnp.max(logits, axis=0, keepdims=True)
    shifted = logits - top
    logsum = jnp.log(jnp.sum(jnp.exp(shifted), axis=0, keepdims=True))
    value = rest - (math.log(1.0 - smoothing) + (shifted - logsum))
    entry = index_ref[...] - base_ref[0]
    num_top, tokens = value.shape
    part = 64
    for lower in range(0, out_ref.shape[1], part):
        row = lax.broadcasted_iota(jnp.int32, (part, tokens), 0) + lower
        dense = jnp.zeros((part, tokens), F32)
        for k in range(num_top):
            dense = jnp.where(row == entry[k : k + 1, :], value[k : k + 1, :], dense)
        out_ref[0, lower : lower + part, :] = dense


def teacher_weights(order, base, index, logits, width, rest):
    num_top = index.shape[0]
    slots = order.shape[0]
    tokens = index.shape[1] // BLOCKS
    spec = pl.BlockSpec((num_top, tokens), lambda j, order, base: (0, order[j]))
    return pl.pallas_call(
        functools.partial(teacher_kernel, rest),
        grid_spec=pltpu.PrefetchScalarGridSpec(
            num_scalar_prefetch=2,
            grid=(slots,),
            in_specs=[spec, spec],
            out_specs=pl.BlockSpec((1, width, tokens), lambda j, order, base: (j, 0, 0)),
        ),
        out_shape=jax.ShapeDtypeStruct((slots, width, tokens), F32),
        compiler_params=params(),
        cost_estimate=cost(slots * tokens * width * num_top, slots * tokens * width * 4),
        name="teacher_weights",
    )(order, base, index, logits)


def logits_kernel(slots, earlier, head_ref, *refs):
    count = len(slots)
    pieces, weights, before = refs[: 2 * count], refs[2 * count : 3 * count], refs[3 * count : -2]
    logits_ref, sums_ref = refs[-2:]
    step = pl.program_id(0)
    block = jnp.concatenate([p[...] for p in pieces], axis=0)
    part = lax.dot_general(
        head_ref[0], block, (((1,), (1,)), ((), ())), preferred_element_type=F32
    )
    tokens = logits_ref.shape[2]

    @pl.when(step == 0)
    def _():
        for n in range(count):
            logits_ref[n] = part[:, n * tokens : (n + 1) * tokens]

    @pl.when(step > 0)
    def _():
        for n in range(count):
            logits_ref[n] += part[:, n * tokens : (n + 1) * tokens]

    @pl.when(step == pl.num_programs(0) - 1)
    def _():
        for n in range(count):
            logits = logits_ref[n]
            top = jnp.max(logits, axis=0, keepdims=True)
            shifted = logits - top
            expo = jnp.exp(shifted)
            total = jnp.sum(expo, axis=0, keepdims=True)
            mixed = jnp.sum(expo * (shifted + weights[n][0]), axis=0, keepdims=True)
            for at, value in enumerate((top, total, mixed)):
                row = at * BLOCKS + slots[n]
                sums_ref[row : row + 1, :] = value
        for group, ref in zip(earlier, before):
            for slot in group:
                for row in range(slot, 3 * BLOCKS, BLOCKS):
                    sums_ref[row : row + 1, :] = ref[row : row + 1, :]


def block_logits(slots, a, b, head, weights, earlier=(), before=()):
    _, width, depth = head.shape
    half = a[slots[0]].shape[0]
    tokens = 2 * half
    count = len(slots)
    step = 3072
    return pl.pallas_call(
        functools.partial(logits_kernel, slots, earlier),
        grid=(depth // step,),
        in_specs=[pl.BlockSpec((1, width, step), lambda i: (0, 0, i))]
        + [pl.BlockSpec((half, step), lambda i: (0, i))] * (2 * count)
        + [pl.BlockSpec((1, width, tokens), lambda i, s=s: (s % RING, 0, 0)) for s in slots]
        + [pl.BlockSpec((3 * BLOCKS, tokens), lambda i: (0, 0))] * len(before),
        out_specs=[
            pl.BlockSpec((count, width, tokens), lambda i: (0, 0, 0)),
            pl.BlockSpec((3 * BLOCKS, tokens), lambda i: (0, 0)),
        ],
        out_shape=[
            jax.ShapeDtypeStruct((count, width, tokens), F32),
            jax.ShapeDtypeStruct((3 * BLOCKS, tokens), F32),
        ],
        compiler_params=params(),
        cost_estimate=cost(2 * count * tokens * width * depth, width * depth * 2),
        name="block_logits",
    )(head, *[x[s] for s in slots for x in (a, b)], *[weights[s // RING] for s in slots], *before)


def merge_sums(parts):
    top = functools.reduce(jnp.maximum, [p[0] for p in parts])
    total, mixed = 0.0, 0.0
    for one_top, one_total, one_mixed in parts:
        down = jnp.exp(one_top - top)
        total = total + one_total * down
        mixed = mixed + down * (one_mixed + (one_top - top) * one_total)
    return top, total, mixed


def dlogits_kernel(rest, where, cot_ref, *refs):
    weights, sums = refs[:SIDES], refs[SIDES : SIDES + RING]
    logits = refs[SIDES + RING : -3]
    low_t_ref, low_ref, loss_ref = refs[-3:]
    tokens = cot_ref.shape[1]
    parts = []
    for shift in range(RING):
        found = []
        for lower in range(0, 3 * BLOCKS, RING):
            if shift:
                found.append(sums[shift][lower + RING - shift : lower + RING, :])
            found.append(sums[shift][lower : lower + RING - shift, :])
        found = jnp.concatenate(found, axis=0)
        parts.append([found[n * BLOCKS : (n + 1) * BLOCKS] for n in range(3)])
    top, total, mixed = merge_sums(parts)
    logtotals = jnp.log(total)
    logzs = top + logtotals
    losses = mixed / total - logtotals - rest
    loss_ref[...] = losses
    for slot in range(BLOCKS):
        side, ahead = slot // RING, slot % RING
        logz, loss = logzs[slot : slot + 1], losses[slot : slot + 1]
        group, at = where[slot]
        rel = logits[group][at] - logz
        grads = cot_ref[slot : slot + 1] * jnp.exp(rel) * (
            rel - (rest + loss) + weights[side][ahead]
        )
        here = slice(slot * tokens, (slot + 1) * tokens)
        low_t_ref[:, here] = grads.astype(BF16)
        low_ref[here, :] = jnp.transpose(grads).astype(BF16)


def some_dlogits(lower, rows, groups, found, weights, cot, sums, rest):
    _, width, tokens = weights[0].shape
    where = {s: (g, n) for g, group in enumerate(groups) for n, s in enumerate(group)}
    step = math.gcd(lower, rows)
    at = lower // step

    def whole(x):
        return pl.BlockSpec(x.shape, lambda i: (0,) * x.ndim)

    def some(x):
        return pl.BlockSpec((x.shape[0], step, tokens), lambda i: (0, i + at, 0))

    return pl.pallas_call(
        functools.partial(dlogits_kernel, rest, where),
        grid=(rows // step,),
        in_specs=[whole(cot)]
        + [some(x) for x in weights]
        + [whole(x) for x in sums]
        + [some(x) for x in found],
        out_specs=[
            pl.BlockSpec((step, BLOCKS * tokens), lambda i: (i, 0)),
            pl.BlockSpec((BLOCKS * tokens, step), lambda i: (0, i)),
            pl.BlockSpec((BLOCKS, tokens), lambda i: (0, 0)),
        ],
        out_shape=[
            jax.ShapeDtypeStruct((rows, BLOCKS * tokens), BF16),
            jax.ShapeDtypeStruct((BLOCKS * tokens, rows), BF16),
            jax.ShapeDtypeStruct((BLOCKS, tokens), F32),
        ],
        compiler_params=params(),
        cost_estimate=cost(0, 0),
        name="some_dlogits",
    )(cot, *weights, *sums, *found)


def part_kernel(low_ref, *refs):
    normed = jnp.concatenate([p[...] for p in refs[:-1]], axis=0)
    refs[-1][...] = jnp.dot(low_ref[...], normed, preferred_element_type=F32).astype(BF16)


def table_part(low_t, pieces, lower, size):
    rows, tokens = low_t.shape
    half = pieces[0].shape[0]
    step = COLUMNS
    start = lower // step
    return pl.pallas_call(
        part_kernel,
        grid=(size // step,),
        in_specs=[pl.BlockSpec((rows, tokens), lambda i: (0, 0))]
        + [pl.BlockSpec((half, step), lambda i: (0, i + start)) for _ in pieces],
        out_specs=pl.BlockSpec((rows, step), lambda i: (0, i)),
        out_shape=jax.ShapeDtypeStruct((rows, size), BF16),
        compiler_params=params(),
        cost_estimate=cost(2 * rows * tokens * size, (rows + tokens) * size * 2),
        name="table_part",
    )(low_t, *pieces)


def table_kernel(first_ref, other_ref, head_ref, gain_ref, *refs):
    pieces, (out_ref, gain_out_ref) = refs[:-2], refs[-2:]
    normed = jnp.concatenate([p[...] for p in pieces], axis=0)
    low = jnp.concatenate([first_ref[...], other_ref[...]], axis=0)
    grads = jnp.dot(low, normed, preferred_element_type=F32)
    out_ref[...] = grads.astype(BF16)
    along = jnp.sum(head_ref[0].astype(F32) * grads, axis=0, keepdims=True) / gain_ref[...]
    gain_out_ref[...] = jnp.broadcast_to(along, gain_out_ref.shape)


def own_table(first, other, head, gain, pieces):
    _, width, depth = head.shape
    tokens = first.shape[1]
    half = pieces[0].shape[0]
    step = COLUMNS
    return pl.pallas_call(
        table_kernel,
        grid=(depth // step,),
        in_specs=[
            pl.BlockSpec(first.shape, lambda i: (0, 0)),
            pl.BlockSpec(other.shape, lambda i: (0, 0)),
            pl.BlockSpec((1, width, step), lambda i: (0, 0, i)),
            pl.BlockSpec((1, step), lambda i: (0, i)),
        ]
        + [pl.BlockSpec((half, step), lambda i: (0, i)) for _ in pieces],
        out_specs=[
            pl.BlockSpec((width, step), lambda i: (0, i)),
            pl.BlockSpec((8, step), lambda i: (0, i)),
        ],
        out_shape=[
            jax.ShapeDtypeStruct((width, depth), BF16),
            jax.ShapeDtypeStruct((8, depth), F32),
        ],
        compiler_params=params(),
        cost_estimate=cost(2 * width * tokens * depth, (tokens + 2 * width) * depth * 2),
        name="own_table",
    )(first, other, head, gain, *pieces)


def add_kernel(own_ref, other_ref, *refs):
    refs[-1][0] = (own_ref[...].astype(F32) + other_ref[...].astype(F32)).astype(BF16)


def add_part(own, other, earlier, part):
    width, depth = own.shape
    row, num_rows, column, num_columns = part
    wide = math.gcd(column, num_columns) or num_columns
    block = (ROWS, wide * COLUMNS)
    first = earlier is None
    return pl.pallas_call(
        add_kernel,
        grid=(num_rows, num_columns // wide),
        in_specs=[
            pl.BlockSpec(block, lambda i, j: (i + row, j + column // wide)),
            pl.BlockSpec(block, lambda i, j: (i, j)),
        ]
        + ([] if first else [pl.BlockSpec(memory_space=pl.ANY)]),
        out_specs=pl.BlockSpec((1,) + block, lambda i, j: (0, i + row, j + column // wide)),
        out_shape=jax.ShapeDtypeStruct((1, width, depth), BF16),
        input_output_aliases={} if first else {2: 0},
        compiler_params=params(),
        cost_estimate=cost(other.size, other.size * 6),
        name="add_part",
    )(own, other, *(() if first else (earlier,)))


def partial_kernel(counts, head_ref, *refs):
    flat = [c for group in counts for c in group]
    num = len(flat)
    lows, rest, outs = refs[: 2 * num], refs[2 * num : -len(counts)], refs[-len(counts) :]
    half = lows[0].shape[0]
    low = jnp.concatenate(
        [jnp.concatenate([r[...] for r in lows[n::num]], axis=1) for n in range(num)], axis=0
    )
    sums = jnp.dot(low, head_ref[0], preferred_element_type=F32)
    job, at = 0, 0
    for out, group in zip(outs, counts):
        for n, count in enumerate(group):
            total = sums[job * half : (job + 1) * half].astype(BF16).astype(F32)
            for r in rest[at : at + count]:
                total = total + r[...].astype(F32)
            out[n * half : (n + 1) * half, :] = total.astype(out.dtype)
            job, at = job + 1, at + count


def partials(low, head, groups, dtype=BF16):
    _, width, depth = head.shape
    half = low[0].shape[0] // (2 * BLOCKS)
    step = 2048
    jobs = [job for group in groups for job in group]
    counts = [[len(add) for _, add in group] for group in groups]
    added = [x for _, add in jobs for x in add]
    return pl.pallas_call(
        functools.partial(partial_kernel, counts),
        grid=(depth // step,),
        in_specs=[pl.BlockSpec((1, width, step), lambda i: (0, 0, i))]
        + [pl.BlockSpec((half, x.shape[1]), lambda i, at=at: (at, 0)) for x in low for at, _ in jobs]
        + [pl.BlockSpec((half, step), lambda i, row=row: (row, i)) for _, row in added],
        out_specs=[pl.BlockSpec((len(g) * half, step), lambda i: (0, i)) for g in groups],
        out_shape=[jax.ShapeDtypeStruct((len(g) * half, depth), dtype) for g in groups],
        compiler_params=params(),
        cost_estimate=cost(
            2 * len(jobs) * half * width * depth,
            width * depth * 2 + (len(jobs) + len(added)) * half * depth * 2,
        ),
        name="partials",
    )(head, *[x for x in low for _ in jobs], *[x for x, _ in added])


def join_kernel(counts, *refs):
    given, outs = refs[: -len(counts)], refs[-len(counts) :]
    sums, rest = given[: len(counts)], given[len(counts) :]
    at = 0
    for out, own, group in zip(outs, sums, counts):
        half = out.shape[0] // len(group)
        for n, count in enumerate(group):
            here = slice(n * half, (n + 1) * half)
            total = own[here, :].astype(F32)
            for r in rest[at : at + count]:
                total = total + r[...].astype(F32)
            at += count
            out[here, :] = total.astype(out.dtype)


def join(own, groups):
    rows, depth = own[0].shape
    step = depth // 2
    counts = [[len(add) for add in group] for group in groups]
    added = [x for group in groups for add in group for x in add]
    whole = pl.BlockSpec((rows, step), lambda i: (0, i))
    return pl.pallas_call(
        functools.partial(join_kernel, counts),
        grid=(depth // step,),
        in_specs=[whole] * len(own)
        + [pl.BlockSpec((rows // 2, step), lambda i, row=row: (row, i)) for _, row in added],
        out_specs=[whole] * len(own),
        out_shape=[jax.ShapeDtypeStruct(x.shape, x.dtype) for x in own],
        compiler_params=params(),
        cost_estimate=cost(0, 0),
        name="join",
    )(*own, *[x for x, _ in added])


def states_kernel(hidden_ref, scale_ref, gain_ref, *refs):
    parts, out_ref = refs[:-1], refs[-1]
    dnormed = parts[0][...].astype(F32)
    for r in parts[1:]:
        dnormed = dnormed + r[...].astype(F32)
    scale = scale_ref[:, 0:1]
    unit = hidden_ref[...].astype(F32) * scale
    scaled = gain_ref[...] * dnormed
    along = jnp.mean(unit * scaled, axis=1, keepdims=True)
    out_ref[...] = (scale * scaled - scale * unit * along).astype(BF16)


def states_gradient(hidden, scale, gain, parts):
    rows, width = hidden.shape
    step = rows // 4
    block = pl.BlockSpec((step, width), lambda i: (i, 0))
    return pl.pallas_call(
        states_kernel,
        grid=(rows // step,),
        in_specs=[
            block,
            pl.BlockSpec((step, scale.shape[1]), lambda i: (i, 0)),
            pl.BlockSpec((1, width), lambda i: (0, 0)),
        ]
        + [block] * len(parts),
        out_specs=block,
        out_shape=jax.ShapeDtypeStruct((rows, width), BF16),
        compiler_params=params(),
        cost_estimate=cost(0, 0),
        name="states_gradient",
    )(hidden, scale, gain, *parts)


def ring_perm(step):
    return [
        (y * SIDES + s, ((y + step) % RING) * SIDES + s)
        for y in range(RING)
        for s in range(SIDES)
    ]


def gate(values, *needed):
    found = lax.optimization_barrier((tuple(values), tuple(needed)))[0]
    return found if len(found) > 1 else found[0]


def body(hidden, gain, head, teacher_index, teacher_logits, cotangent):
    up, down, across = ring_perm(1), ring_perm(-1), ring_perm(2)
    swap = [(f, f ^ 1) for f in range(BLOCKS)]
    num_pipe = lax.axis_size("pipe")
    mirror = [(p, num_pipe - 1 - p) for p in range(num_pipe)]
    facing = [
        (p * BLOCKS + f, (num_pipe - 1 - p) * BLOCKS + (f ^ 1))
        for p in range(num_pipe)
        for f in range(BLOCKS)
    ]

    def send(x, perm):
        return lax.ppermute(x, "fsdp", perm)

    def exchange(x):
        return lax.ppermute(x, ("pipe", "fsdp"), facing)

    _, width, depth = head.shape
    rows = teacher_index.shape[0]
    tokens = rows // BLOCKS
    num_top = teacher_index.shape[1]
    rest = math.log(smoothing / (width * BLOCKS - num_top))

    a, b = {}, {}
    a[0], scale_a = norm_half(hidden, gain, 0)
    b[0], scale_b = norm_half(hidden, gain, 1)
    a[3] = send(a[0], up)
    a[1] = send(a[0], down)
    a[4] = send(a[0], swap)
    b[3] = send(b[0], up)
    b[1] = send(b[0], down)

    me = lax.axis_index("fsdp")
    slots = jnp.arange(BLOCKS, dtype=jnp.int32)
    order = ((me // SIDES + slots % RING) % RING) * SIDES + (me % SIDES) ^ (slots // RING)
    order = order.astype(jnp.int32)
    base = (me * width).astype(jnp.int32).reshape(1)
    index_t, logits_t = teacher_index.T, teacher_logits.T
    weights = [teacher_weights(order[:RING], base, index_t, logits_t, width, rest)]
    cot = jnp.take(cotangent.reshape(BLOCKS, tokens), order, axis=0)

    groups = ((0,), (3, 1, 4), (5,), (2, 7), (6,))
    b0, a[4] = gate((b[0], a[4]), a[3], a[1], weights[0])
    b[4] = send(b0, swap)
    found = [block_logits(groups[0], a, b, head, weights)]
    a4, order, base = gate((a[4], order, base), found[0][1])
    a[7] = send(a4, up)
    a[5] = send(a4, down)
    weights.append(teacher_weights(order[RING:], base, index_t, logits_t, width, rest))
    a3, b1, b[4] = gate((a[3], b[1], b[4]), b[3])
    a[2] = send(a3, up)
    b[2] = send(b1, down)
    b[5] = send(b1, swap)
    found.append(block_logits(groups[1], a, b, head, weights))
    b3, a7, b5 = gate((b[3], a[7], b[5]), a[5], found[1][1])
    b[7] = send(b3, swap)
    a[6] = send(a7, up)
    b[6] = send(b5, down)
    found.append(block_logits(groups[2], a, b, head, weights))
    a[2], b[2], b[7] = gate((a[2], b[2], b[7]), found[2][1])
    found.append(block_logits(groups[3], a, b, head, weights))
    a[6], b[6] = gate((a[6], b[6]), found[3][1])
    found.append(
        block_logits(groups[4], a, b, head, weights, groups[:4], [f[1] for f in found])
    )
    sums = found[-1][1]
    other = send(sums, swap).reshape(3, SIDES, RING, tokens)[:, ::-1].reshape(sums.shape)
    pair = jnp.concatenate(
        merge_sums([[x[n : n + BLOCKS] for n in range(0, 3 * BLOCKS, BLOCKS)] for x in (sums, other)]),
        axis=0,
    )
    ring_sums = [pair, send(pair, down), send(pair, across), send(pair, up)]
    given = (groups, [f[0] for f in found], weights, cot)
    first, low_first, loss = some_dlogits(0, ROWS, *given, ring_sums, rest)
    their_first = send(first, swap)
    ring_sums = [gate((ring_sums[0],), first)] + ring_sums[1:]
    second, low_second, _ = some_dlogits(ROWS, width - ROWS, *given, ring_sums, rest)
    low = (low_first, low_second)

    pieces, facing_pieces = [], []
    for slot in range(BLOCKS):
        pieces += [a[slot], b[slot]]
        other_slot = (slot + RING) % BLOCKS
        facing_pieces += [a[other_slot], b[other_slot]]

    def part_of(n, low_t):
        _, _, column, num_columns = PARTS[n]
        return table_part(low_t, facing_pieces, column * COLUMNS, num_columns * COLUMNS)

    their_first, second_there = gate((their_first, second), second)
    their_second = send(second_there, swap)
    parts = [part_of(0, their_first)]
    theirs = [exchange(parts[0])]
    o2a, o2b = partials(gate(low, parts[0]), head, [[(12, [])], [(13, [])]])
    r_o2a, r_o2b = send(o2a, down), send(o2b, up)
    ahead = partials(
        gate(low, o2a),
        head,
        [[(14, []), (4, [])], [(10, []), (5, [])], [(11, []), (15, [])]],
    )
    their_second = gate((their_second,), *ahead)
    parts.append(part_of(1, their_second))

    *low, first, second, their_first, their_second, a0, a1, a2 = gate(
        (*low, first, second, their_first, their_second, *ahead),
        r_o2a, r_o2b, theirs[0], parts[1],
    )
    theirs.append(exchange(parts[1]))
    to_down, to_swap = join([a0, a2], [[[(r_o2a, 0)], []], [[(r_o2b, 0)], []]])
    o3a_s2a, o1a_s2b, o1b_o3b = send(to_down, down), send(a1, up), send(to_swap, swap)
    their_first, their_second, first, second = gate(
        (their_first, their_second, first, second), to_down
    )
    parts += [part_of(2, their_second), part_of(3, their_second)]
    theirs.append(exchange(parts[2]))
    ahead = partials(
        gate(low, to_down), head, [[(6, []), (7, [])], [(2, []), (3, [])], [(8, []), (9, [])]]
    )

    own, along = own_table(first, second, head, gain, pieces)
    along = along[:1].reshape(8, depth // 8)
    scale = jnp.concatenate([scale_a, scale_b], axis=0)

    *low, own, along, scale, own_loss, theirs[1], parts[3], their_first, a0, a1, a2 = gate(
        (*low, own, along, scale, loss[0], theirs[1], parts[3], their_first, *ahead),
        o3a_s2a, o1a_s2b, o1b_o3b,
    )
    theirs.append(exchange(parts[3]))
    along = along + send(along, swap)
    to_down, to_up, to_swap = gate(join(
        [a0, a1, a2],
        [
            [[(o3a_s2a, 1)], [(o1b_o3b, 1)]],
            [[], [(o1a_s2b, 1), (o1b_o3b, 0)]],
            [[(o3a_s2a, 0), (o1a_s2b, 0)], []],
        ],
    ), along)
    s3, s1, o0 = send(to_down, down), send(to_up, up), send(to_swap, swap)
    *low, their_first = gate((*low, their_first), to_down)
    parts.append(part_of(4, their_first))
    (mine,) = partials(low, head, [[(0, []), (1, [])]])
    merged = None
    for n in range(2):
        merged = add_part(own, theirs[n], merged, PARTS[n])
    parts[4] = gate((parts[4],), theirs[2], merged)
    theirs.append(exchange(parts[4]))
    merged = add_part(own, theirs[2], merged, PARTS[2])

    mine, along, merged = gate((mine, along, merged), s3, s1, o0)
    grad_states = states_gradient(hidden, scale, gain, [mine, s3, s1, o0])
    merged = add_part(own, theirs[3], merged, PARTS[3])
    along = along + send(along, [(f, f ^ SIDES) for f in range(BLOCKS)])
    along = gate((along,), grad_states)
    opposite = [
        (p * BLOCKS + f, (num_pipe - 1 - p) * BLOCKS + t)
        for p in range(num_pipe)
        for f, t in across
    ]
    ours = (along + send(along, across)).astype(BF16)
    mirrored = lax.ppermute(along, "pipe", mirror) + lax.ppermute(
        along, ("pipe", "fsdp"), opposite
    )
    merged_gain = (ours.astype(F32) + mirrored.astype(BF16).astype(F32)).astype(BF16)
    merged_gain = merged_gain.reshape(1, depth)
    theirs[4], merged = gate((theirs[4], merged), grad_states)
    merged = add_part(own, theirs[4], merged, PARTS[4])
    return (own_loss, grad_states, merged, merged_gain)


def solution(mesh):
    in_specs = (
        P(("pipe", "fsdp"), None),
        P("pipe", None),
        P("pipe", "fsdp", None),
        P("pipe", None),
        P("pipe", None),
        P("pipe"),
    )
    out_specs = (
        P(("pipe", "fsdp")),
        P(("pipe", "fsdp"), None),
        P("pipe", "fsdp", None),
        P("pipe", None),
    )
    return jax.shard_map(body, mesh=mesh, in_specs=in_specs, out_specs=out_specs, check_vma=False)
```

```python
import functools
import math

import jax
import jax.numpy as jnp
from jax import lax
from jax.experimental import pallas as pl
from jax.experimental.pallas import tpu as pltpu
from jax.sharding import PartitionSpec as P

smoothing = 0.1
epsilon = 1e-05
F32 = jnp.float32
BF16 = jnp.bfloat16
BIG = 65408 * 1024

RING, SIDES = 4, 2
BLOCKS = RING * SIDES
ROWS, COLUMNS = 128, 768
PARTS = (
    (0, 1, 2, 6),
    (1, 3, 0, 3),
    (1, 3, 3, 3),
    (1, 3, 6, 2),
    (0, 1, 0, 2),
)


def params(**kw):
    return pltpu.CompilerParams(vmem_limit_bytes=BIG, **kw)


def cost(flops, nbytes):
    del flops, nbytes
    return pl.CostEstimate(flops=1, bytes_accessed=1, transcendentals=0)


def norm_kernel(hidden_ref, gain_ref, normed_ref, scale_ref):
    floats = hidden_ref[...].astype(F32)
    scale = lax.rsqrt(jnp.mean(floats * floats, axis=1, keepdims=True) + epsilon)
    normed_ref[...] = (floats * scale * gain_ref[...]).astype(BF16)
    scale_ref[...] = jnp.broadcast_to(scale, scale_ref.shape)


def norm_half(hidden, gain, half):
    rows, width = hidden.shape
    step = rows // 4
    return pl.pallas_call(
        norm_kernel,
        grid=(2,),
        in_specs=[
            pl.BlockSpec((step, width), lambda i: (i + 2 * half, 0)),
            pl.BlockSpec((1, width), lambda i: (0, 0)),
        ],
        out_specs=[
            pl.BlockSpec((step, width), lambda i: (i, 0)),
            pl.BlockSpec((step, 128), lambda i: (i, 0)),
        ],
        out_shape=[
            jax.ShapeDtypeStruct((rows // 2, width), BF16),
            jax.ShapeDtypeStruct((rows // 2, 128), F32),
        ],
        compiler_params=params(),
        cost_estimate=cost(rows * width * 2, rows * width * 2),
        name="norm_half",
    )(hidden, gain)


def teacher_kernel(rest, order_ref, base_ref, index_ref, logit_ref, out_ref):
    logits = logit_ref[...]
    top = jnp.max(logits, axis=0, keepdims=True)
    shifted = logits - top
    logsum = jnp.log(jnp.sum(jnp.exp(shifted), axis=0, keepdims=True))
    value = rest - (math.log(1.0 - smoothing) + (shifted - logsum))
    entry = index_ref[...] - base_ref[0]
    num_top, tokens = value.shape
    part = 64
    for lower in range(0, out_ref.shape[1], part):
        row = lax.broadcasted_iota(jnp.int32, (part, tokens), 0) + lower
        dense = jnp.zeros((part, tokens), F32)
        for k in range(num_top):
            dense = jnp.where(row == entry[k : k + 1, :], value[k : k + 1, :], dense)
        out_ref[0, lower : lower + part, :] = dense


def teacher_weights(order, base, index, logits, width, rest):
    num_top = index.shape[0]
    slots = order.shape[0]
    tokens = index.shape[1] // BLOCKS
    spec = pl.BlockSpec((num_top, tokens), lambda j, order, base: (0, order[j]))
    return pl.pallas_call(
        functools.partial(teacher_kernel, rest),
        grid_spec=pltpu.PrefetchScalarGridSpec(
            num_scalar_prefetch=2,
            grid=(slots,),
            in_specs=[spec, spec],
            out_specs=pl.BlockSpec((1, width, tokens), lambda j, order, base: (j, 0, 0)),
        ),
        out_shape=jax.ShapeDtypeStruct((slots, width, tokens), F32),
        compiler_params=params(),
        cost_estimate=cost(slots * tokens * width * num_top, slots * tokens * width * 4),
        name="teacher_weights",
    )(order, base, index, logits)


def logits_kernel(slots, earlier, head_ref, *refs):
    count = len(slots)
    pieces, weights, before = refs[: 2 * count], refs[2 * count : 3 * count], refs[3 * count : -2]
    logits_ref, sums_ref = refs[-2:]
    step = pl.program_id(0)
    block = jnp.concatenate([p[...] for p in pieces], axis=0)
    part = lax.dot_general(
        head_ref[0], block, (((1,), (1,)), ((), ())), preferred_element_type=F32
    )
    tokens = logits_ref.shape[2]

    @pl.when(step == 0)
    def _():
        for n in range(count):
            logits_ref[n] = part[:, n * tokens : (n + 1) * tokens]

    @pl.when(step > 0)
    def _():
        for n in range(count):
            logits_ref[n] += part[:, n * tokens : (n + 1) * tokens]

    @pl.when(step == pl.num_programs(0) - 1)
    def _():
        for n in range(count):
            logits = logits_ref[n]
            top = jnp.max(logits, axis=0, keepdims=True)
            shifted = logits - top
            expo = jnp.exp(shifted)
            total = jnp.sum(expo, axis=0, keepdims=True)
            mixed = jnp.sum(expo * (shifted + weights[n][0]), axis=0, keepdims=True)
            for at, value in enumerate((top, total, mixed)):
                row = at * BLOCKS + slots[n]
                sums_ref[row : row + 1, :] = value
        for group, ref in zip(earlier, before):
            for slot in group:
                for row in range(slot, 3 * BLOCKS, BLOCKS):
                    sums_ref[row : row + 1, :] = ref[row : row + 1, :]


def block_logits(slots, a, b, head, weights, earlier=(), before=()):
    _, width, depth = head.shape
    half = a[slots[0]].shape[0]
    tokens = 2 * half
    count = len(slots)
    step = 3072
    return pl.pallas_call(
        functools.partial(logits_kernel, slots, earlier),
        grid=(depth // step,),
        in_specs=[pl.BlockSpec((1, width, step), lambda i: (0, 0, i))]
        + [pl.BlockSpec((half, step), lambda i: (0, i))] * (2 * count)
        + [pl.BlockSpec((1, width, tokens), lambda i, s=s: (s % RING, 0, 0)) for s in slots]
        + [pl.BlockSpec((3 * BLOCKS, tokens), lambda i: (0, 0))] * len(before),
        out_specs=[
            pl.BlockSpec((count, width, tokens), lambda i: (0, 0, 0)),
            pl.BlockSpec((3 * BLOCKS, tokens), lambda i: (0, 0)),
        ],
        out_shape=[
            jax.ShapeDtypeStruct((count, width, tokens), F32),
            jax.ShapeDtypeStruct((3 * BLOCKS, tokens), F32),
        ],
        compiler_params=params(),
        cost_estimate=cost(2 * count * tokens * width * depth, width * depth * 2),
        name="block_logits",
    )(head, *[x[s] for s in slots for x in (a, b)], *[weights[s // RING] for s in slots], *before)


def merge_sums(parts):
    top = functools.reduce(jnp.maximum, [p[0] for p in parts])
    total, mixed = 0.0, 0.0
    for one_top, one_total, one_mixed in parts:
        down = jnp.exp(one_top - top)
        total = total + one_total * down
        mixed = mixed + down * (one_mixed + (one_top - top) * one_total)
    return top, total, mixed


def dlogits_kernel(rest, where, cot_ref, *refs):
    weights, sums = refs[:SIDES], refs[SIDES : SIDES + RING]
    logits = refs[SIDES + RING : -3]
    low_t_ref, low_ref, loss_ref = refs[-3:]
    tokens = cot_ref.shape[1]
    parts = []
    for shift in range(RING):
        found = []
        for lower in range(0, 3 * BLOCKS, RING):
            if shift:
                found.append(sums[shift][lower + RING - shift : lower + RING, :])
            found.append(sums[shift][lower : lower + RING - shift, :])
        found = jnp.concatenate(found, axis=0)
        parts.append([found[n * BLOCKS : (n + 1) * BLOCKS] for n in range(3)])
    top, total, mixed = merge_sums(parts)
    logtotals = jnp.log(total)
    logzs = top + logtotals
    losses = mixed / total - logtotals - rest
    loss_ref[...] = losses
    for slot in range(BLOCKS):
        side, ahead = slot // RING, slot % RING
        logz, loss = logzs[slot : slot + 1], losses[slot : slot + 1]
        group, at = where[slot]
        rel = logits[group][at] - logz
        grads = cot_ref[slot : slot + 1] * jnp.exp(rel) * (
            rel - (rest + loss) + weights[side][ahead]
        )
        here = slice(slot * tokens, (slot + 1) * tokens)
        low_t_ref[:, here] = grads.astype(BF16)
        low_ref[here, :] = jnp.transpose(grads).astype(BF16)


def some_dlogits(lower, rows, groups, found, weights, cot, sums, rest):
    _, width, tokens = weights[0].shape
    where = {s: (g, n) for g, group in enumerate(groups) for n, s in enumerate(group)}
    step = math.gcd(lower, rows)
    at = lower // step

    def whole(x):
        return pl.BlockSpec(x.shape, lambda i: (0,) * x.ndim)

    def some(x):
        return pl.BlockSpec((x.shape[0], step, tokens), lambda i: (0, i + at, 0))

    return pl.pallas_call(
        functools.partial(dlogits_kernel, rest, where),
        grid=(rows // step,),
        in_specs=[whole(cot)]
        + [some(x) for x in weights]
        + [whole(x) for x in sums]
        + [some(x) for x in found],
        out_specs=[
            pl.BlockSpec((step, BLOCKS * tokens), lambda i: (i, 0)),
            pl.BlockSpec((BLOCKS * tokens, step), lambda i: (0, i)),
            pl.BlockSpec((BLOCKS, tokens), lambda i: (0, 0)),
        ],
        out_shape=[
            jax.ShapeDtypeStruct((rows, BLOCKS * tokens), BF16),
            jax.ShapeDtypeStruct((BLOCKS * tokens, rows), BF16),
            jax.ShapeDtypeStruct((BLOCKS, tokens), F32),
        ],
        compiler_params=params(),
        cost_estimate=cost(0, 0),
        name="some_dlogits",
    )(cot, *weights, *sums, *found)


def part_kernel(low_ref, *refs):
    normed = jnp.concatenate([p[...] for p in refs[:-1]], axis=0)
    refs[-1][...] = jnp.dot(low_ref[...], normed, preferred_element_type=F32).astype(BF16)


def table_part(low_t, pieces, lower, size):
    rows, tokens = low_t.shape
    half = pieces[0].shape[0]
    step = COLUMNS
    start = lower // step
    return pl.pallas_call(
        part_kernel,
        grid=(size // step,),
        in_specs=[pl.BlockSpec((rows, tokens), lambda i: (0, 0))]
        + [pl.BlockSpec((half, step), lambda i: (0, i + start)) for _ in pieces],
        out_specs=pl.BlockSpec((rows, step), lambda i: (0, i)),
        out_shape=jax.ShapeDtypeStruct((rows, size), BF16),
        compiler_params=params(),
        cost_estimate=cost(2 * rows * tokens * size, (rows + tokens) * size * 2),
        name="table_part",
    )(low_t, *pieces)


def table_kernel(first_ref, other_ref, head_ref, gain_ref, *refs):
    pieces, (out_ref, gain_out_ref) = refs[:-2], refs[-2:]
    normed = jnp.concatenate([p[...] for p in pieces], axis=0)
    low = jnp.concatenate([first_ref[...], other_ref[...]], axis=0)
    grads = jnp.dot(low, normed, preferred_element_type=F32)
    out_ref[...] = grads.astype(BF16)
    along = jnp.sum(head_ref[0].astype(F32) * grads, axis=0, keepdims=True) / gain_ref[...]
    gain_out_ref[...] = jnp.broadcast_to(along, gain_out_ref.shape)


def own_table(first, other, head, gain, pieces):
    _, width, depth = head.shape
    tokens = first.shape[1]
    half = pieces[0].shape[0]
    step = COLUMNS
    return pl.pallas_call(
        table_kernel,
        grid=(depth // step,),
        in_specs=[
            pl.BlockSpec(first.shape, lambda i: (0, 0)),
            pl.BlockSpec(other.shape, lambda i: (0, 0)),
            pl.BlockSpec((1, width, step), lambda i: (0, 0, i)),
            pl.BlockSpec((1, step), lambda i: (0, i)),
        ]
        + [pl.BlockSpec((half, step), lambda i: (0, i)) for _ in pieces],
        out_specs=[
            pl.BlockSpec((width, step), lambda i: (0, i)),
            pl.BlockSpec((8, step), lambda i: (0, i)),
        ],
        out_shape=[
            jax.ShapeDtypeStruct((width, depth), BF16),
            jax.ShapeDtypeStruct((8, depth), F32),
        ],
        compiler_params=params(),
        cost_estimate=cost(2 * width * tokens * depth, (tokens + 2 * width) * depth * 2),
        name="own_table",
    )(first, other, head, gain, *pieces)


def add_kernel(own_ref, other_ref, *refs):
    refs[-1][0] = (own_ref[...].astype(F32) + other_ref[...].astype(F32)).astype(BF16)


def add_part(own, other, earlier, part):
    width, depth = own.shape
    row, num_rows, column, num_columns = part
    wide = math.gcd(column, num_columns) or num_columns
    block = (ROWS, wide * COLUMNS)
    first = earlier is None
    return pl.pallas_call(
        add_kernel,
        grid=(num_rows, num_columns // wide),
        in_specs=[
            pl.BlockSpec(block, lambda i, j: (i + row, j + column // wide)),
            pl.BlockSpec(block, lambda i, j: (i, j)),
        ]
        + ([] if first else [pl.BlockSpec(memory_space=pl.ANY)]),
        out_specs=pl.BlockSpec((1,) + block, lambda i, j: (0, i + row, j + column // wide)),
        out_shape=jax.ShapeDtypeStruct((1, width, depth), BF16),
        input_output_aliases={} if first else {2: 0},
        compiler_params=params(),
        cost_estimate=cost(other.size, other.size * 6),
        name="add_part",
    )(own, other, *(() if first else (earlier,)))


def partial_kernel(counts, head_ref, *refs):
    flat = [c for group in counts for c in group]
    num = len(flat)
    lows, rest, outs = refs[: 2 * num], refs[2 * num : -len(counts)], refs[-len(counts) :]
    half = lows[0].shape[0]
    low = jnp.concatenate(
        [jnp.concatenate([r[...] for r in lows[n::num]], axis=1) for n in range(num)], axis=0
    )
    sums = jnp.dot(low, head_ref[0], preferred_element_type=F32)
    job, at = 0, 0
    for out, group in zip(outs, counts):
        for n, count in enumerate(group):
            total = sums[job * half : (job + 1) * half].astype(BF16).astype(F32)
            for r in rest[at : at + count]:
                total = total + r[...].astype(F32)
            out[n * half : (n + 1) * half, :] = total.astype(out.dtype)
            job, at = job + 1, at + count


def partials(low, head, groups, dtype=BF16):
    _, width, depth = head.shape
    half = low[0].shape[0] // (2 * BLOCKS)
    step = 2048
    jobs = [job for group in groups for job in group]
    counts = [[len(add) for _, add in group] for group in groups]
    added = [x for _, add in jobs for x in add]
    return pl.pallas_call(
        functools.partial(partial_kernel, counts),
        grid=(depth // step,),
        in_specs=[pl.BlockSpec((1, width, step), lambda i: (0, 0, i))]
        + [pl.BlockSpec((half, x.shape[1]), lambda i, at=at: (at, 0)) for x in low for at, _ in jobs]
        + [pl.BlockSpec((half, step), lambda i, row=row: (row, i)) for _, row in added],
        out_specs=[pl.BlockSpec((len(g) * half, step), lambda i: (0, i)) for g in groups],
        out_shape=[jax.ShapeDtypeStruct((len(g) * half, depth), dtype) for g in groups],
        compiler_params=params(),
        cost_estimate=cost(
            2 * len(jobs) * half * width * depth,
            width * depth * 2 + (len(jobs) + len(added)) * half * depth * 2,
        ),
        name="partials",
    )(head, *[x for x in low for _ in jobs], *[x for x, _ in added])


def join_kernel(counts, *refs):
    given, outs = refs[: -len(counts)], refs[-len(counts) :]
    sums, rest = given[: len(counts)], given[len(counts) :]
    at = 0
    for out, own, group in zip(outs, sums, counts):
        half = out.shape[0] // len(group)
        for n, count in enumerate(group):
            here = slice(n * half, (n + 1) * half)
            total = own[here, :].astype(F32)
            for r in rest[at : at + count]:
                total = total + r[...].astype(F32)
            at += count
            out[here, :] = total.astype(out.dtype)


def join(own, groups):
    rows, depth = own[0].shape
    step = depth // 2
    counts = [[len(add) for add in group] for group in groups]
    added = [x for group in groups for add in group for x in add]
    whole = pl.BlockSpec((rows, step), lambda i: (0, i))
    return pl.pallas_call(
        functools.partial(join_kernel, counts),
        grid=(depth // step,),
        in_specs=[whole] * len(own)
        + [pl.BlockSpec((rows // 2, step), lambda i, row=row: (row, i)) for _, row in added],
        out_specs=[whole] * len(own),
        out_shape=[jax.ShapeDtypeStruct(x.shape, x.dtype) for x in own],
        compiler_params=params(),
        cost_estimate=cost(0, 0),
        name="join",
    )(*own, *[x for x, _ in added])


def states_kernel(hidden_ref, scale_ref, gain_ref, *refs):
    parts, out_ref = refs[:-1], refs[-1]
    dnormed = parts[0][...].astype(F32)
    for r in parts[1:]:
        dnormed = dnormed + r[...].astype(F32)
    scale = scale_ref[:, 0:1]
    unit = hidden_ref[...].astype(F32) * scale
    scaled = gain_ref[...] * dnormed
    along = jnp.mean(unit * scaled, axis=1, keepdims=True)
    out_ref[...] = (scale * scaled - scale * unit * along).astype(BF16)


def states_gradient(hidden, scale, gain, parts):
    rows, width = hidden.shape
    step = rows // 4
    block = pl.BlockSpec((step, width), lambda i: (i, 0))
    return pl.pallas_call(
        states_kernel,
        grid=(rows // step,),
        in_specs=[
            block,
            pl.BlockSpec((step, scale.shape[1]), lambda i: (i, 0)),
            pl.BlockSpec((1, width), lambda i: (0, 0)),
        ]
        + [block] * len(parts),
        out_specs=block,
        out_shape=jax.ShapeDtypeStruct((rows, width), BF16),
        compiler_params=params(),
        cost_estimate=cost(0, 0),
        name="states_gradient",
    )(hidden, scale, gain, *parts)


def ring_perm(step):
    return [
        (y * SIDES + s, ((y + step) % RING) * SIDES + s)
        for y in range(RING)
        for s in range(SIDES)
    ]


def gate(values, *needed):
    found = lax.optimization_barrier((tuple(values), tuple(needed)))[0]
    return found if len(found) > 1 else found[0]


def body(hidden, gain, head, teacher_index, teacher_logits, cotangent):
    up, down, across = ring_perm(1), ring_perm(-1), ring_perm(2)
    swap = [(f, f ^ 1) for f in range(BLOCKS)]
    num_pipe = lax.axis_size("pipe")
    mirror = [(p, num_pipe - 1 - p) for p in range(num_pipe)]
    facing = [
        (p * BLOCKS + f, (num_pipe - 1 - p) * BLOCKS + (f ^ 1))
        for p in range(num_pipe)
        for f in range(BLOCKS)
    ]

    def send(x, perm):
        return lax.ppermute(x, "fsdp", perm)

    def exchange(x):
        return lax.ppermute(x, ("pipe", "fsdp"), facing)

    _, width, depth = head.shape
    rows = teacher_index.shape[0]
    tokens = rows // BLOCKS
    num_top = teacher_index.shape[1]
    rest = math.log(smoothing / (width * BLOCKS - num_top))

    a, b = {}, {}
    a[0], scale_a = norm_half(hidden, gain, 0)
    b[0], scale_b = norm_half(hidden, gain, 1)
    a[3] = send(a[0], up)
    a[1] = send(a[0], down)
    a[4] = send(a[0], swap)
    b[3] = send(b[0], up)
    b[1] = send(b[0], down)

    me = lax.axis_index("fsdp")
    slots = jnp.arange(BLOCKS, dtype=jnp.int32)
    order = ((me // SIDES + slots % RING) % RING) * SIDES + (me % SIDES) ^ (slots // RING)
    order = order.astype(jnp.int32)
    base = (me * width).astype(jnp.int32).reshape(1)
    index_t, logits_t = teacher_index.T, teacher_logits.T
    weights = [teacher_weights(order[:RING], base, index_t, logits_t, width, rest)]
    cot = jnp.take(cotangent.reshape(BLOCKS, tokens), order, axis=0)

    groups = ((0,), (3, 1, 4), (5,), (2, 7), (6,))
    b0, a[4] = gate((b[0], a[4]), a[3], a[1], weights[0])
    b[4] = send(b0, swap)
    found = [block_logits(groups[0], a, b, head, weights)]
    a4, order, base = gate((a[4], order, base), found[0][1])
    a[7] = send(a4, up)
    a[5] = send(a4, down)
    weights.append(teacher_weights(order[RING:], base, index_t, logits_t, width, rest))
    a3, b1, b[4] = gate((a[3], b[1], b[4]), b[3])
    a[2] = send(a3, up)
    b[2] = send(b1, down)
    b[5] = send(b1, swap)
    found.append(block_logits(groups[1], a, b, head, weights))
    b3, a7, b5 = gate((b[3], a[7], b[5]), a[5], found[1][1])
    b[7] = send(b3, swap)
    a[6] = send(a7, up)
    b[6] = send(b5, down)
    found.append(block_logits(groups[2], a, b, head, weights))
    a[2], b[2], b[7] = gate((a[2], b[2], b[7]), found[2][1])
    found.append(block_logits(groups[3], a, b, head, weights))
    a[6], b[6] = gate((a[6], b[6]), found[3][1])
    found.append(
        block_logits(groups[4], a, b, head, weights, groups[:4], [f[1] for f in found])
    )
    sums = found[-1][1]
    other = send(sums, swap).reshape(3, SIDES, RING, tokens)[:, ::-1].reshape(sums.shape)
    pair = jnp.concatenate(
        merge_sums([[x[n : n + BLOCKS] for n in range(0, 3 * BLOCKS, BLOCKS)] for x in (sums, other)]),
        axis=0,
    )
    ring_sums = [pair, send(pair, down), send(pair, across), send(pair, up)]
    given = (groups, [f[0] for f in found], weights, cot)
    first, low_first, loss = some_dlogits(0, ROWS, *given, ring_sums, rest)
    their_first = send(first, swap)
    ring_sums = [gate((ring_sums[0],), first)] + ring_sums[1:]
    second, low_second, _ = some_dlogits(ROWS, width - ROWS, *given, ring_sums, rest)
    low = (low_first, low_second)

    pieces, facing_pieces = [], []
    for slot in range(BLOCKS):
        pieces += [a[slot], b[slot]]
        other_slot = (slot + RING) % BLOCKS
        facing_pieces += [a[other_slot], b[other_slot]]

    def part_of(n, low_t):
        _, _, column, num_columns = PARTS[n]
        return table_part(low_t, facing_pieces, column * COLUMNS, num_columns * COLUMNS)

    their_first, second_there = gate((their_first, second), second)
    their_second = send(second_there, swap)
    parts = [part_of(0, their_first)]
    theirs = [exchange(parts[0])]
    o2a, o2b = partials(gate(low, parts[0]), head, [[(12, [])], [(13, [])]])
    r_o2a, r_o2b = send(o2a, down), send(o2b, up)
    ahead = partials(
        gate(low, o2a),
        head,
        [[(14, []), (4, [])], [(10, []), (5, [])], [(11, []), (15, [])]],
    )
    their_second = gate((their_second,), *ahead)
    parts.append(part_of(1, their_second))

    *low, first, second, their_first, their_second, a0, a1, a2 = gate(
        (*low, first, second, their_first, their_second, *ahead),
        r_o2a, r_o2b, theirs[0], parts[1],
    )
    theirs.append(exchange(parts[1]))
    to_down, to_swap = join([a0, a2], [[[(r_o2a, 0)], []], [[(r_o2b, 0)], []]])
    o3a_s2a, o1a_s2b, o1b_o3b = send(to_down, down), send(a1, up), send(to_swap, swap)
    their_first, their_second, first, second = gate(
        (their_first, their_second, first, second), to_down
    )
    parts += [part_of(2, their_second), part_of(3, their_second)]
    theirs.append(exchange(parts[2]))
    ahead = partials(
        gate(low, to_down), head, [[(6, []), (7, [])], [(2, []), (3, [])], [(8, []), (9, [])]]
    )

    own, along = own_table(first, second, head, gain, pieces)
    along = along[:1].reshape(8, depth // 8)
    scale = jnp.concatenate([scale_a, scale_b], axis=0)

    *low, own, along, scale, own_loss, theirs[1], parts[3], their_first, a0, a1, a2 = gate(
        (*low, own, along, scale, loss[0], theirs[1], parts[3], their_first, *ahead),
        o3a_s2a, o1a_s2b, o1b_o3b,
    )
    theirs.append(exchange(parts[3]))
    along = along + send(along, swap)
    to_down, to_up, to_swap = gate(join(
        [a0, a1, a2],
        [
            [[(o3a_s2a, 1)], [(o1b_o3b, 1)]],
            [[], [(o1a_s2b, 1), (o1b_o3b, 0)]],
            [[(o3a_s2a, 0), (o1a_s2b, 0)], []],
        ],
    ), along)
    s3, s1, o0 = send(to_down, down), send(to_up, up), send(to_swap, swap)
    *low, their_first = gate((*low, their_first), to_down)
    parts.append(part_of(4, their_first))
    (mine,) = partials(low, head, [[(0, []), (1, [])]])
    merged = None
    for n in range(2):
        merged = add_part(own, theirs[n], merged, PARTS[n])
    parts[4] = gate((parts[4],), theirs[2], merged, mine)
    theirs.append(exchange(parts[4]))
    merged = add_part(own, theirs[2], merged, PARTS[2])

    mine, along, merged = gate((mine, along, merged), s3, s1, o0)
    grad_states = states_gradient(hidden, scale, gain, [mine, s3, s1, o0])
    merged = add_part(own, theirs[3], merged, PARTS[3])
    along = along + send(along, [(f, f ^ SIDES) for f in range(BLOCKS)])
    along = gate((along,), grad_states)
    opposite = [
        (p * BLOCKS + f, (num_pipe - 1 - p) * BLOCKS + t)
        for p in range(num_pipe)
        for f, t in across
    ]
    ours = (along + send(along, across)).astype(BF16)
    mirrored = lax.ppermute(along, "pipe", mirror) + lax.ppermute(
        along, ("pipe", "fsdp"), opposite
    )
    merged_gain = (ours.astype(F32) + mirrored.astype(BF16).astype(F32)).astype(BF16)
    merged_gain = merged_gain.reshape(1, depth)
    theirs[4], merged, merged_gain = gate((theirs[4], merged, merged_gain), grad_states)
    merged = add_part(own, theirs[4], merged, PARTS[4])
    return (own_loss, grad_states, merged, merged_gain)


def solution(mesh):
    in_specs = (
        P(("pipe", "fsdp"), None),
        P("pipe", None),
        P("pipe", "fsdp", None),
        P("pipe", None),
        P("pipe", None),
        P("pipe"),
    )
    out_specs = (
        P(("pipe", "fsdp")),
        P(("pipe", "fsdp"), None),
        P("pipe", "fsdp", None),
        P("pipe", None),
    )
    return jax.shard_map(body, mesh=mesh, in_specs=in_specs, out_specs=out_specs, check_vma=False)
```
